128 devices in a mesh: rep: 16 (over y_lo, z, core), tp: 8 (over y_hi, x).
Axes of the slice: x: 4, y: 4 (y_hi: 2, y_lo: 2; y = y_hi * 2 + y_lo), z: 4, core: 2. Of those that a mesh axis runs over, the one named last changes fastest.
Arguments:
- queries: bfloat16 [512, 8192], P('rep', 'tp'), may hold values from -5.5 to 5.5
- new_token_kv: bfloat16 [512, 2048], P('rep', 'tp'), may hold values from -5 to 5
- resident_cache: bfloat16 [512, 384, 2048], P('rep', None, 'tp'), may hold values from -5.5 to 5.5
- resident_lengths: int32 [16, 32], P('rep'), may hold values from 1 to 383, 7660 in all within a row
- new_caches: bfloat16 [256, 8, 128, 512], P('rep', 'tp'), may hold values from -5.5 to 5.5
- new_lengths: int32 [16, 16], P('rep'), may hold values from 1 to 256, 2560 in all within a row
- handoff: int32 [16, 16, 2], P('rep'), may hold values from 0 to 31, as said below
- out_weight: bfloat16 [8192, 8192], P('tp'), may hold values from -0.1875 to 0.1875
Outputs:
- attended: bfloat16 [512, 8192], P('rep')
- updated_cache: bfloat16 [512, 384, 2048], P('rep', None, 'tp')
The draws below stay inside these ranges and needn't reach their ends.
Inputs may be any that keep to these rules, and one draw needn't show every extreme that they name: handoff[g, i] = (decode group, row) of request i of group g. No group hands more than 2 requests to one decode group; one decode group receives exactly 2 from every group; the rows named for one decode group are distinct.
All inputs are finite; a program needn't handle non-finite values.
Results may differ from the reference program's by a relative error of at most 0.008.
Values may be sent and summed in bfloat16 or wider, within the bound.
A program may use at most 128 MiB of HBM per device.

```python
import math
import jax
import jax.numpy as jnp
import numpy as np
from jax import lax

D = 8192
QH = 64
KVH = 8
HEAD = 128
ROWS = 32
P_REQ = 16
LP = 256
L = 384
CAP = 2
GROUPS = 16
PIECES = 8
KVS = 1


def handoff_table(base_key):
    seeded = jax.random.fold_in(base_key, 11)
    key_hot, key_pick, key_rows = jax.random.split(seeded, 3)
    candidates_all = GROUPS * CAP
    hotspot = jax.random.randint(key_hot, (), 0, GROUPS)
    candidate = jnp.arange(candidates_all, dtype=jnp.int32)
    target = candidate // CAP
    within = candidate % CAP

    def one_source(source_key):
        key_first, key_second = jax.random.split(source_key)
        shuffled = jax.random.permutation(key_first, candidates_all)
        position = jnp.argsort(shuffled).astype(jnp.int32)
        priority = jnp.where(target == hotspot, within, CAP + position)
        chosen = jnp.argsort(priority)[:P_REQ].astype(jnp.int32)
        return chosen[jax.random.permutation(key_second, P_REQ)]
    picked = jax.vmap(one_source)(jax.random.split(key_pick, GROUPS))
    groups_of = picked // CAP
    slot_of = picked % CAP

    def one_table(table_key):
        return jax.random.permutation(table_key, ROWS).astype(jnp.int32)
    row_tables = jax.vmap(one_table)(jax.random.split(key_rows, GROUPS))
    source = jnp.arange(GROUPS, dtype=jnp.int32)[:, None]
    rows_of = row_tables[groups_of, source * CAP + slot_of]
    return jnp.stack([groups_of, rows_of], -1).astype(jnp.int32)


def draw_handoff(key, part):
    return handoff_table(key)


def draw_queries(key, part):
    seeded = jax.random.fold_in(key, 1)
    array_shape = (GROUPS * ROWS, KVH, QH // KVH, HEAD)
    values = jax.random.truncated_normal(seeded, -5.0, 5.0, array_shape)
    return values.reshape(GROUPS * ROWS, QH * HEAD).astype(jnp.bfloat16)


def draw_resident_cache(key, part):
    seeded = jax.random.fold_in(key, 2)
    array_shape = (GROUPS * ROWS, L, KVH, 2, HEAD)
    values = jax.random.truncated_normal(seeded, -5.0, 5.0, array_shape)
    return values.reshape(GROUPS * ROWS, L, KVH * 2 * HEAD).astype(jnp.bfloat16)


def draw_new_caches(key, part):
    seeded = jax.random.fold_in(key, 3)
    requests = GROUPS * P_REQ
    array_shape = (requests, KVH, LP, 2, HEAD)
    values = jax.random.truncated_normal(seeded, -5.0, 5.0, array_shape)
    pair_count = PIECES // 2
    heads_per_piece = 2 * KVH // PIECES
    values = values.reshape(requests, pair_count, heads_per_piece, 2, LP // 2, 2, HEAD)
    values = values.transpose(0, 1, 3, 4, 2, 5, 6)
    return values.reshape(requests, PIECES, LP // 2, heads_per_piece * 2 * HEAD).astype(jnp.bfloat16)


def level_of(key, dims, cuts, low, top_value):
    gain = 1.0
    for dim, blocks in cuts:
        steps = jax.random.uniform(jax.random.fold_in(jax.random.fold_in(key, 6), dim), (blocks,), jnp.float32, low / len(cuts), top_value / len(cuts))
        gain = gain * jnp.repeat(jnp.exp(steps), dims[dim] // blocks).reshape((-1,) + (1,) * (len(dims) - 1 - dim))
    return gain


def length_profile(count, total, reach, skew):
    weights = [(1 << 20) // math.isqrt(standing ** skew) + 1 for standing in range(2, count + 1)]
    rest, given = total - reach - (count - 1), [1] * (count - 1)
    while rest > 0:
        free = [i for i in range(count - 1) if given[i] < reach]
        pool, budget = sum([weights[i] for i in free]), rest
        for i in free:
            addition = min(reach - given[i], max(1, budget * weights[i] // pool), rest)
            given[i] = given[i] + addition
            rest = rest - addition
    return np.array([reach] + given)


def ragged(rng, number_of, total, limit, skew):
    if number_of == 2:
        one = jax.random.randint(rng, (), max(1, total - limit), min(limit, total - 1) + 1)
        return jnp.stack([one, total - one])
    lengths = jnp.asarray(length_profile(number_of, total, limit, skew), jnp.int32)
    couples = (number_of - 1) // 2
    source_of, sink = lengths[1:1 + 2 * couples:2], lengths[2:2 + 2 * couples:2]
    margin = jnp.minimum(source_of - 1, limit - sink)
    moved = jax.random.randint(jax.random.fold_in(rng, 1), (couples,), 0, 1 << 20) % (margin + 1)
    lengths = lengths.at[1:1 + 2 * couples:2].set(source_of - moved).at[2:2 + 2 * couples:2].set(sink + moved)
    return lengths[jax.random.permutation(jax.random.fold_in(rng, 2), number_of)]


def centred(stream_key, shape, spread, bound, cuts=(), kind=jnp.bfloat16):
    entries = spread * jax.random.normal(stream_key, shape, jnp.float32)
    if cuts:
        entries = entries * level_of(stream_key, shape, cuts, -0.22, 0.18)
    return jnp.clip(entries, -bound, bound).astype(kind)


def setup_inputs(seed: int = 0) -> dict:
    key_list = jax.random.split(jax.random.key(seed), 9)
    queries = draw_queries(jax.random.fold_in(key_list[8], 71), 0)
    new_token_kv = centred(key_list[1], (GROUPS * ROWS, KVH * 2 * HEAD), 1.0, 5.0, ((0, 16), (1, 8)))
    resident_cache = draw_resident_cache(jax.random.fold_in(key_list[8], 71), 0)
    resident_lengths = jax.vmap(lambda own: ragged(own, ROWS, ROWS * (L - 1) * 5 // 8, L - 1, 2))(jax.random.split(key_list[3], GROUPS)).reshape((GROUPS, ROWS)).astype(jnp.int32)
    new_caches = draw_new_caches(jax.random.fold_in(key_list[8], 71), 0)
    new_lengths = jax.vmap(lambda own: ragged(own, P_REQ, P_REQ * LP * 5 // 8, LP, 2))(jax.random.split(key_list[5], GROUPS)).reshape((GROUPS, P_REQ)).astype(jnp.int32)
    handoff = draw_handoff(jax.random.fold_in(key_list[8], 71), 0)
    out_weight = centred(key_list[7], (QH * HEAD, D), (HEAD * 8) ** -0.5, 0.1875, ((0, 8),))
    return dict(queries=queries, new_token_kv=new_token_kv, resident_cache=resident_cache, resident_lengths=resident_lengths, new_caches=new_caches, new_lengths=new_lengths, handoff=handoff, out_weight=out_weight)


NEG_FILL = -1e30


def partial_softmax(query_rows, key_rows, value_rows, valid_mask):
    scores = jnp.einsum('nkgd,nlkd->nkgl', query_rows, key_rows.astype(jnp.float32)) * (HEAD ** -0.5)
    allowed = valid_mask[:, None, None, :]
    maxima = jnp.max(jnp.where(allowed, scores, NEG_FILL), axis=3)
    shifted = jnp.where(allowed, scores, maxima[..., None]) - maxima[..., None]
    exp_scores = jnp.where(allowed, jnp.exp(shifted), 0.0)
    weights = lax.optimization_barrier(exp_scores.astype(jnp.bfloat16)).astype(jnp.float32)
    totals = jnp.sum(weights, axis=3)
    accumulated = jnp.einsum('nkgl,nlkd->nkgd', weights, value_rows.astype(jnp.float32))
    return maxima, totals, accumulated


def combine_partials(pieces_list, own_score, own_value):
    running_peak = own_score
    for maxima, totals, accumulated in pieces_list:
        running_peak = jnp.maximum(running_peak, maxima)
    own_weight = jnp.exp(own_score - running_peak)
    numerator = own_weight[..., None] * own_value[:, :, None, :]
    denominator = own_weight
    for maxima, totals, accumulated in pieces_list:
        factor = jnp.exp(maxima - running_peak)
        numerator = numerator + factor[..., None] * accumulated
        denominator = denominator + factor * totals
    return numerator / denominator[..., None]


def reference(queries, new_token_kv, resident_cache, resident_lengths, new_caches, new_lengths, handoff, out_weight):
    requests = GROUPS * P_REQ
    per_kv = QH // KVH
    pair_count = PIECES // 2
    heads_per_piece = 2 * KVS
    half_len = LP // 2
    canonical = new_caches.reshape(requests, pair_count, 2, half_len, heads_per_piece, 2, HEAD)
    canonical = canonical.transpose(0, 2, 3, 1, 4, 5, 6).reshape(requests, LP, KVH, 2, HEAD)
    flat_handoff = handoff.reshape(requests, 2)
    target = flat_handoff[:, 0] * ROWS + flat_handoff[:, 1]
    owner_of = jnp.full((GROUPS * ROWS,), -1, jnp.int32).at[target].set(jnp.arange(requests, dtype=jnp.int32))
    request_lengths = new_lengths.reshape(requests)

    def one_group(group_id):
        row_start = (group_id * ROWS).astype(jnp.int32)
        query_rows = lax.dynamic_slice_in_dim(queries, row_start, ROWS, 0).astype(jnp.float32).reshape(ROWS, KVH, per_kv, HEAD)
        own_pair = lax.dynamic_slice_in_dim(new_token_kv, row_start, ROWS, 0)
        own_view = own_pair.reshape(ROWS, KVH, 2, HEAD).astype(jnp.float32)
        own_score = jnp.einsum('nkgd,nkd->nkg', query_rows, own_view[:, :, 0, :]) * (HEAD ** -0.5)
        own_value = own_view[:, :, 1, :]
        cache_rows = lax.dynamic_slice_in_dim(resident_cache, row_start, ROWS, 0)
        cache_view = cache_rows.reshape(ROWS, L, KVH, 2, HEAD)
        lengths_here = lax.dynamic_index_in_dim(resident_lengths, group_id, 0, keepdims=False)
        positions = jnp.arange(L, dtype=jnp.int32)
        resident_part = partial_softmax(query_rows, cache_view[:, :, :, 0, :], cache_view[:, :, :, 1, :], positions[None, :] < lengths_here[:, None])
        resident_out = combine_partials([resident_part], own_score, own_value)
        owners_here = lax.dynamic_slice_in_dim(owner_of, row_start, ROWS, 0)
        replaced = owners_here >= 0
        chosen = jnp.maximum(owners_here, 0)
        arrived = canonical[chosen]
        arrived_len = jnp.where(replaced, request_lengths[chosen], 0)
        offsets = jnp.arange(half_len, dtype=jnp.int32)
        lower_part = partial_softmax(query_rows, arrived[:, :half_len, :, 0, :], arrived[:, :half_len, :, 1, :], offsets[None, :] < arrived_len[:, None])
        upper_part = partial_softmax(query_rows, arrived[:, half_len:, :, 0, :], arrived[:, half_len:, :, 1, :], (offsets + half_len)[None, :] < arrived_len[:, None])
        arrived_out = combine_partials([lower_part, upper_part], own_score, own_value)
        attention_rows = jnp.where(replaced[:, None, None, None], arrived_out, resident_out).reshape(ROWS, QH * HEAD).astype(jnp.bfloat16)
        attended = jnp.dot(attention_rows, out_weight, preferred_element_type=jnp.float32).astype(jnp.bfloat16)
        slot_ids = positions[None, :, None]
        own_flat = own_pair[:, None, :]
        resident_kept = jnp.where(slot_ids == lengths_here[:, None, None], own_flat, cache_rows)
        padded = jnp.pad(arrived.reshape(ROWS, LP, KVH * 2 * HEAD), ((0, 0), (0, L - LP), (0, 0)))
        installed = jnp.where(slot_ids == arrived_len[:, None, None], own_flat, jnp.where(slot_ids < arrived_len[:, None, None], padded, jnp.zeros_like(padded)))
        updated = jnp.where(replaced[:, None, None], installed, resident_kept)
        return attended, updated

    attended, updated = lax.map(one_group, jnp.arange(GROUPS, dtype=jnp.int32))
    return attended.reshape(GROUPS * ROWS, D), updated.reshape(GROUPS * ROWS, L, KVH * 2 * HEAD)
```

```python
import functools

import jax
import jax.numpy as jnp
from jax import lax
from jax.experimental import pallas as pl
from jax.experimental.pallas import tpu as pltpu
from jax.sharding import PartitionSpec as P

HEAD = 128
CAP = 2
NEG_FILL = -1e30
MESH = pl.DeviceIdType.MESH

REP_STEPS = [
    (y, z, c)
    for z in (1, 3, 2, 0)
    for y in (1, 0)
    for c in (0, 1)
    if (y, z, c) != (0, 0, 0)
]
TP_STEPS = [(h, x) for x in (2, 1, 3, 0) for h in (1, 0) if (h, x) != (0, 0)]


def rep_at(rep, step, sign):
    y, z, c = rep // 8, (rep // 2) % 4, rep % 2
    dy, dz, dc = step
    return ((y + dy) % 2) * 8 + ((z + sign * dz + 4) % 4) * 2 + (c + dc) % 2


def tp_at(tp, step, sign):
    h, x = tp // 4, tp % 4
    dh, dx = step
    return ((h + dh) % 2) * 4 + (x + sign * dx + 4) % 4


def handoff_kernel(
    hand_s, hand_ref, len_ref, caches, arrived, hand_all, len_all,
    own, other, packed, own_sem, pair_send, pair_recv, send, recv, stay, mh_send, mh_recv, ml_send, ml_recv,
):
    rep, tp = lax.axis_index("rep"), lax.axis_index("tp")
    parity = tp % 2
    partner = tp + 1 - 2 * parity
    width = own.shape[2]
    half = own.shape[1]
    count = own.shape[0]
    mine = pl.ds(pl.multiple_of(parity * width, width), width)
    theirs = pl.ds(pl.multiple_of((1 - parity) * width, width), width)
    load = pltpu.make_async_copy(caches.at[:, 0, :, mine], own, own_sem)
    load.start()

    barrier = pltpu.get_barrier_semaphore()
    for step in REP_STEPS:
        pl.semaphore_signal(barrier, inc=1, device_id=(rep_at(rep, step, -1), tp), device_id_type=MESH)
    pl.semaphore_signal(barrier, inc=1, device_id=(rep, partner), device_id_type=MESH)
    pl.semaphore_wait(barrier, len(REP_STEPS) + 1)

    pair = pltpu.make_async_remote_copy(
        src_ref=caches.at[:, 0, :, theirs], dst_ref=other, send_sem=pair_send, recv_sem=pair_recv,
        device_id=(rep, partner), device_id_type=MESH,
    )
    pair.start()
    copies = []
    for k, step in enumerate(REP_STEPS):
        to = (rep_at(rep, step, 1), tp)
        for src, dst, s, r in (
            (hand_ref.at[0], hand_all.at[rep], mh_send, mh_recv),
            (len_ref, len_all.at[rep], ml_send, ml_recv),
        ):
            copy = pltpu.make_async_remote_copy(
                src_ref=src, dst_ref=dst, send_sem=s.at[k], recv_sem=r.at[k], device_id=to, device_id_type=MESH
            )
            copy.start()
            copies.append(copy)
    hand_all[rep] = hand_ref[0]
    len_all[rep] = len_ref[...]

    targets = [hand_s[0, i, 0] for i in range(count)]

    def sources(group):
        seen, first, second = jnp.int32(0), jnp.int32(0), jnp.int32(0)
        for i in range(count):
            hit = targets[i] == group
            first = jnp.where(hit & (seen == 0), i, first)
            second = jnp.where(hit & (seen == 1), i, second)
            seen = seen + hit.astype(jnp.int32)
        return first, second

    picks = [sources(rep_at(rep, step, 1)) for step in REP_STEPS]
    picks.append(sources(rep))
    slots = pl.ds(rep * CAP, CAP)
    for phase, held in ((0, own), (1, other)):
        if phase == 0:
            load.wait()
        else:
            pair.wait()
        part = parity if phase == 0 else 1 - parity
        tokens = pl.ds(pl.multiple_of(part * half, half), half)
        for k, step in enumerate(REP_STEPS):
            first, second = picks[k]
            packed[phase, k, 0] = held[first]
            packed[phase, k, 1] = held[second]
            copy = pltpu.make_async_remote_copy(
                src_ref=packed.at[phase, k], dst_ref=arrived.at[slots, tokens, :],
                send_sem=send.at[phase, k], recv_sem=recv.at[phase, k],
                device_id=(rep_at(rep, step, 1), tp), device_id_type=MESH,
            )
            copy.start()
            copies.append(copy)
        k = len(REP_STEPS)
        packed[phase, k, 0] = held[picks[k][0]]
        packed[phase, k, 1] = held[picks[k][1]]
        copy = pltpu.make_async_copy(packed.at[phase, k], arrived.at[slots, tokens, :], stay.at[phase])
        copy.start()
        copies.append(copy)
    for copy in copies:
        copy.wait()


def hand_off(handoff, new_lengths, new_caches):
    count, _, half, wide = new_caches.shape
    width = wide // 2
    groups = lax.axis_size("rep")
    peers = len(REP_STEPS)
    dma = pltpu.SemaphoreType.DMA
    vmem = pl.BlockSpec(memory_space=pltpu.VMEM)
    return pl.pallas_call(
        handoff_kernel,
        out_shape=(
            jax.ShapeDtypeStruct((groups * CAP, 2 * half, width), new_caches.dtype),
            jax.ShapeDtypeStruct((groups,) + handoff.shape[1:], handoff.dtype),
            jax.ShapeDtypeStruct((groups,) + new_lengths.shape, new_lengths.dtype),
        ),
        in_specs=[pl.BlockSpec(memory_space=pltpu.SMEM), vmem, vmem, pl.BlockSpec(memory_space=pl.ANY)],
        out_specs=(pl.BlockSpec(memory_space=pl.ANY), vmem, vmem),
        scratch_shapes=[
            pltpu.VMEM((count, half, width), new_caches.dtype),
            pltpu.VMEM((count, half, width), new_caches.dtype),
            pltpu.VMEM((2, groups, CAP, half, width), new_caches.dtype),
            dma, dma, dma, dma((2, peers)), dma((2, peers)), dma((2,)),
            dma((peers,)), dma((peers,)), dma((peers,)), dma((peers,)),
        ],
        compiler_params=pltpu.CompilerParams(
            collective_id=0, has_side_effects=True, vmem_limit_bytes=24 * 2**20
        ),
        name="hand_off",
    )(handoff, handoff, new_lengths, new_caches)


def project_kernel(rows, weight, out, held, staged, parts, load, rs_send, rs_recv, ag_send, ag_recv):
    rep, tp = lax.axis_index("rep"), lax.axis_index("tp")
    width = staged.shape[2]
    steps = TP_STEPS + [(0, 0)]
    last = len(TP_STEPS)
    loads = []
    for k, step in enumerate(steps):
        at = pl.multiple_of(tp_at(tp, step, 1) * width, width)
        copy = pltpu.make_async_copy(weight.at[:, pl.ds(at, width)], held.at[k], load.at[k])
        copy.start()
        loads.append(copy)
    barrier = pltpu.get_barrier_semaphore()
    for step in TP_STEPS:
        pl.semaphore_signal(barrier, inc=1, device_id=(rep, tp_at(tp, step, -1)), device_id_type=MESH)
    pl.semaphore_wait(barrier, len(TP_STEPS))
    scatter = []
    for k, step in enumerate(TP_STEPS):
        loads[k].wait()
        staged[k] = jnp.dot(rows[...], held[k], preferred_element_type=jnp.float32).astype(staged.dtype)
        copy = pltpu.make_async_remote_copy(
            src_ref=staged.at[k], dst_ref=parts.at[k], send_sem=rs_send.at[k], recv_sem=rs_recv.at[k],
            device_id=(rep, tp_at(tp, step, 1)), device_id_type=MESH,
        )
        copy.start()
        scatter.append(copy)
    loads[last].wait()
    total = jnp.dot(rows[...], held[last], preferred_element_type=jnp.float32)
    for k in range(last):
        scatter[k].wait_recv()
        total = total + parts[k].astype(jnp.float32)
    columns = pl.ds(pl.multiple_of(tp * width, width), width)
    out[:, columns] = total.astype(out.dtype)
    gather = []
    for k, step in enumerate(TP_STEPS):
        copy = pltpu.make_async_remote_copy(
            src_ref=out.at[:, columns], dst_ref=out.at[:, columns], send_sem=ag_send.at[k], recv_sem=ag_recv.at[k],
            device_id=(rep, tp_at(tp, step, 1)), device_id_type=MESH,
        )
        copy.start()
        gather.append(copy)
    for copy in scatter:
        copy.wait_send()
    for copy in gather:
        copy.wait()


def project(rows, weight):
    count, depth = rows.shape
    columns = weight.shape[1]
    shares = lax.axis_size("tp")
    width = columns // shares
    peers = len(TP_STEPS)
    dma = pltpu.SemaphoreType.DMA
    vmem = pl.BlockSpec(memory_space=pltpu.VMEM)
    return pl.pallas_call(
        project_kernel,
        out_shape=jax.ShapeDtypeStruct((count, columns), rows.dtype),
        in_specs=[vmem, pl.BlockSpec(memory_space=pl.ANY)],
        out_specs=vmem,
        scratch_shapes=[
            pltpu.VMEM((shares, depth, width), weight.dtype),
            pltpu.VMEM((peers, count, width), rows.dtype),
            pltpu.VMEM((peers, count, width), rows.dtype),
            dma((shares,)), dma((peers,)), dma((peers,)), dma((peers,)), dma((peers,)),
        ],
        compiler_params=pltpu.CompilerParams(
            collective_id=1, has_side_effects=True, vmem_limit_bytes=32 * 2**20
        ),
        name="project",
    )(rows, weight)


def partial_softmax(query_rows, key_rows, value_rows, valid_mask):
    scores = jnp.einsum(
        "nkgd,nlkd->nkgl", query_rows, key_rows, preferred_element_type=jnp.float32
    ) * HEAD ** (-0.5)
    allowed = valid_mask[:, None, None, :]
    maxima = jnp.max(jnp.where(allowed, scores, NEG_FILL), axis=3)
    shifted = jnp.where(allowed, scores, maxima[..., None]) - maxima[..., None]
    exp_scores = jnp.where(allowed, jnp.exp(shifted), 0.0)
    weights = exp_scores.astype(jnp.bfloat16)
    totals = jnp.sum(weights.astype(jnp.float32), axis=3)
    accumulated = jnp.einsum(
        "nkgl,nlkd->nkgd", weights, value_rows, preferred_element_type=jnp.float32
    )
    return (maxima, totals, accumulated)


def combine_partials(pieces_list, own_score, own_value):
    running_peak = own_score
    for maxima, totals, accumulated in pieces_list:
        running_peak = jnp.maximum(running_peak, maxima)
    own_weight = jnp.exp(own_score - running_peak)
    numerator = own_weight[..., None] * own_value[:, :, None, :]
    denominator = own_weight
    for maxima, totals, accumulated in pieces_list:
        factor = jnp.exp(maxima - running_peak)
        numerator = numerator + factor[..., None] * accumulated
        denominator = denominator + factor * totals
    return numerator / denominator[..., None]


def take_halves(full_heads, query_rows, lengths_of, half_len):
    entry_count = full_heads.shape[0]
    cache_view = full_heads.reshape(entry_count, 2 * half_len, -1, 2, HEAD)
    offsets = jnp.arange(half_len, dtype=jnp.int32)
    lower_part = partial_softmax(
        query_rows,
        cache_view[:, :half_len, :, 0, :],
        cache_view[:, :half_len, :, 1, :],
        offsets[None, :] < lengths_of[:, None],
    )
    upper_part = partial_softmax(
        query_rows,
        cache_view[:, half_len:, :, 0, :],
        cache_view[:, half_len:, :, 1, :],
        (offsets + half_len)[None, :] < lengths_of[:, None],
    )
    return [lower_part, upper_part]


def body(
    queries,
    new_token_kv,
    resident_cache,
    resident_lengths,
    new_caches,
    new_lengths,
    handoff,
    out_weight,
):
    row_count = queries.shape[0]
    cache_len = resident_cache.shape[1]
    piece_width = resident_cache.shape[2]
    kv_here = piece_width // (2 * HEAD)
    per_kv = queries.shape[1] // (HEAD * kv_here)
    half_len = new_caches.shape[2]
    group_count = lax.axis_size("rep")
    entries = group_count * CAP
    query_rows = queries.reshape(row_count, kv_here, per_kv, HEAD)
    own_view = new_token_kv.reshape(row_count, kv_here, 2, HEAD)
    own_score = jnp.einsum(
        "nkgd,nkd->nkg", query_rows, own_view[:, :, 0, :], preferred_element_type=jnp.float32
    ) * HEAD ** (-0.5)
    own_value = own_view[:, :, 1, :].astype(jnp.float32)
    lengths_here = resident_lengths[0]
    positions = jnp.arange(cache_len, dtype=jnp.int32)
    cache_view = resident_cache.reshape(row_count, cache_len, kv_here, 2, HEAD)
    resident_part = partial_softmax(
        query_rows,
        cache_view[:, :, :, 0, :],
        cache_view[:, :, :, 1, :],
        positions[None, :] < lengths_here[:, None],
    )
    resident_out = combine_partials([resident_part], own_score, own_value)
    full_heads, hand_all, len_all = hand_off(handoff, new_lengths, new_caches)
    len_all = len_all[:, 0]
    to_me = hand_all[:, :, 0] == lax.axis_index("rep")
    rank = jnp.cumsum(to_me.astype(jnp.int32), axis=1) - 1
    pick = to_me[:, None, :] & (rank[:, None, :] == jnp.arange(CAP, dtype=jnp.int32)[None, :, None])
    filled = jnp.any(pick, axis=2)
    rows_of = jnp.where(filled, jnp.sum(jnp.where(pick, hand_all[:, None, :, 1], 0), axis=2), -1).reshape(entries)
    lengths_of = jnp.sum(jnp.where(pick, len_all[:, None, :], 0), axis=2).reshape(entries)
    matches_rows = rows_of[:, None] == jnp.arange(row_count, dtype=jnp.int32)[None, :]
    selector = matches_rows.astype(jnp.bfloat16)
    entry_queries = jnp.dot(selector, queries, preferred_element_type=jnp.float32).astype(
        jnp.bfloat16
    )
    entry_queries = entry_queries.reshape(entries, kv_here, per_kv, HEAD)
    entry_own = jnp.dot(selector, new_token_kv, preferred_element_type=jnp.float32).astype(
        jnp.bfloat16
    )
    entry_own = entry_own.reshape(entries, kv_here, 2, HEAD)
    entry_score = jnp.einsum(
        "nkgd,nkd->nkg", entry_queries, entry_own[:, :, 0, :], preferred_element_type=jnp.float32
    ) * HEAD ** (-0.5)
    entry_value = entry_own[:, :, 1, :].astype(jnp.float32)
    pieces_list = take_halves(full_heads, entry_queries, lengths_of, half_len)
    entry_out = combine_partials(pieces_list, entry_score, entry_value).reshape(entries, -1)
    replaced = jnp.any(matches_rows, axis=0)
    entry_index = jnp.sum(
        jnp.where(matches_rows, jnp.arange(entries, dtype=jnp.int32)[:, None], 0), axis=0
    )
    arrived_out = entry_out[entry_index]
    attention_rows = jnp.where(
        replaced[:, None], arrived_out, resident_out.reshape(row_count, -1)
    ).astype(jnp.bfloat16)
    attended = project(attention_rows, out_weight)
    arrived_len = jnp.where(replaced, lengths_of[entry_index], 0)
    padded = jnp.pad(full_heads[entry_index], ((0, 0), (0, cache_len - 2 * half_len), (0, 0)))
    slot_ids = positions[None, :, None]
    own_flat = new_token_kv[:, None, :]
    installed = jnp.where(
        slot_ids == arrived_len[:, None, None],
        own_flat,
        jnp.where(slot_ids < arrived_len[:, None, None], padded, jnp.zeros((), padded.dtype)),
    )
    resident_kept = jnp.where(slot_ids == lengths_here[:, None, None], own_flat, resident_cache)
    updated = jnp.where(replaced[:, None, None], installed, resident_kept)
    return (attended, updated)


def solution(mesh):
    placed = (
        P("rep", "tp"),
        P("rep", "tp"),
        P("rep", None, "tp"),
        P("rep", None),
        P("rep", "tp", None, None),
        P("rep", None),
        P("rep", None, None),
        P("tp", None),
    )
    return jax.shard_map(
        body,
        mesh=mesh,
        in_specs=placed,
        out_specs=(P("rep", None), P("rep", None, "tp")),
        check_vma=False,
    )
```

```python
import functools

import jax
import jax.numpy as jnp
from jax import lax
from jax.experimental import pallas as pl
from jax.experimental.pallas import tpu as pltpu
from jax.sharding import PartitionSpec as P

HEAD = 128
CAP = 2
NEG_FILL = -1e30
SCALE = HEAD ** (-0.5)
MESH = pl.DeviceIdType.MESH
NO_ROW = 32
LEN_UNIT = 64
RES_PARTS = 4

REP_STEPS = [
    (y, z, c)
    for z in (1, 3, 2, 0)
    for y in (1, 0)
    for c in (0, 1)
    if (y, z, c) != (0, 0, 0)
]
TP_STEPS = [(h, x) for x in (2, 1, 3, 0) for h in (1, 0) if (h, x) != (0, 0)]


def rep_at(rep, step, sign):
    y, z, c = rep // 8, (rep // 2) % 4, rep % 2
    dy, dz, dc = step
    return ((y + dy) % 2) * 8 + ((z + sign * dz + 4) % 4) * 2 + (c + dc) % 2


def tp_at(tp, step, sign):
    h, x = tp // 4, tp % 4
    dh, dx = step
    return ((h + dh) % 2) * 4 + (x + sign * dx + 4) % 4


def iota(shape, dim):
    return lax.broadcasted_iota(jnp.int32, shape, dim)


def contract_last(a, b):
    return lax.dot_general(a, b, (((1,), (1,)), ((), ())), preferred_element_type=jnp.float32)


def contract_first(a, b):
    return lax.dot_general(a, b, (((0,), (0,)), ((), ())), preferred_element_type=jnp.float32)


def attend_pair(query_pair, kv_a, kv_b, limits):
    low = iota(query_pair.shape, 0) < 8
    zero = jnp.zeros_like(query_pair)
    blocks = jnp.concatenate([jnp.where(low, query_pair, zero), jnp.where(low, zero, query_pair)], axis=1)
    keys = jnp.concatenate([kv_a[:, :HEAD], kv_b[:, :HEAD]], axis=1)
    values = jnp.concatenate([kv_a[:, HEAD:], kv_b[:, HEAD:]], axis=1)
    scores = contract_last(blocks.astype(jnp.bfloat16), keys) * SCALE
    allowed = iota(scores.shape, 1) < limits
    peak = jnp.max(jnp.where(allowed, scores, NEG_FILL), axis=1, keepdims=True)
    weights = jnp.where(allowed, jnp.exp(jnp.where(allowed, scores, peak) - peak), 0.0).astype(jnp.bfloat16)
    total = jnp.sum(weights.astype(jnp.float32), axis=1, keepdims=True)
    both = jnp.dot(weights, values, preferred_element_type=jnp.float32)
    return peak, total, jnp.where(low, both[:, :HEAD], both[:, HEAD:])


def combine(peak, total, acc, own_score, own_value):
    top = jnp.maximum(peak, own_score)
    own_weight, factor = jnp.exp(own_score - top), jnp.exp(peak - top)
    return (own_weight * own_value + factor * acc) / (own_weight + factor * total)


def layer_kernel(
    hand, new_len, res_len, queries, own_kv, resident, caches, weight,
    attended, arrived_out, meta_all,
    own, other, packed, arrived, res, held, meta_send, q3, eq3, own_k, own_v, own_s, selector, rows3, entry_out,
    staged, parts,
    own_sem, pair_send, pair_recv, send, recv, stay, meta_s, meta_r, res_sem, out_sem, load, rs_send, rs_recv, ag_send, ag_recv,
):
    rep, tp = lax.axis_index("rep"), lax.axis_index("tp")
    parity = tp % 2
    partner = tp + 1 - 2 * parity
    count, half, width = own.shape
    row_count = res.shape[0]
    peers = len(REP_STEPS)
    mine = pl.ds(pl.multiple_of(parity * width, width), width)
    theirs = pl.ds(pl.multiple_of((1 - parity) * width, width), width)
    own_load = pltpu.make_async_copy(caches.at[:, 0, :, mine], own, own_sem)
    own_load.start()
    res_loads = []
    part_rows = row_count // RES_PARTS
    for k in range(RES_PARTS):
        rows = pl.ds(k * part_rows, part_rows)
        copy = pltpu.make_async_copy(resident.at[rows], res.at[rows], res_sem.at[k])
        copy.start()
        res_loads.append(copy)

    barrier = pltpu.get_barrier_semaphore()
    for step in REP_STEPS:
        pl.semaphore_signal(barrier, inc=1, device_id=(rep_at(rep, step, -1), tp), device_id_type=MESH)
    for step in TP_STEPS:
        pl.semaphore_signal(barrier, inc=1, device_id=(rep, tp_at(tp, step, -1)), device_id_type=MESH)

    targets = [hand[0, i, 0] for i in range(count)]

    def slot_picks(group):
        seen, first, second = jnp.int32(0), jnp.int32(0), jnp.int32(0)
        for i in range(count):
            hit = targets[i] == group
            first = jnp.where(hit & (seen == 0), i, first)
            second = jnp.where(hit & (seen == 1), i, second)
            seen = seen + hit.astype(jnp.int32)
        return first, second, seen

    def code_of(pick, filled):
        return jnp.where(filled, hand[0, pick, 1] + LEN_UNIT * new_len[0, pick], NO_ROW)

    picks = []
    for k, step in enumerate(REP_STEPS + [(0, 0, 0)]):
        first, second, seen = slot_picks(rep_at(rep, step, 1))
        picks.append((first, second))
        meta_send[k, 0:8, :] = jnp.full((8, HEAD), code_of(first, seen > 0), jnp.int32)
        meta_send[k, 8:16, :] = jnp.full((8, HEAD), code_of(second, seen > 1), jnp.int32)
    meta_all[rep] = meta_send[peers]
    pl.semaphore_wait(barrier, len(REP_STEPS) + len(TP_STEPS))

    pair = pltpu.make_async_remote_copy(
        src_ref=caches.at[:, 0, :, theirs], dst_ref=other, send_sem=pair_send, recv_sem=pair_recv,
        device_id=(rep, partner), device_id_type=MESH,
    )
    pair.start()
    metas = []
    for k, step in enumerate(REP_STEPS):
        copy = pltpu.make_async_remote_copy(
            src_ref=meta_send.at[k], dst_ref=meta_all.at[rep], send_sem=meta_s.at[k], recv_sem=meta_r.at[k],
            device_id=(rep_at(rep, step, 1), tp), device_id_type=MESH,
        )
        copy.start()
        metas.append(copy)

    slots = pl.ds(rep * CAP, CAP)
    bulk = [[], []]

    def send_phase(phase, from_ref):
        part = parity if phase == 0 else 1 - parity
        tokens = pl.ds(pl.multiple_of(part * half, half), half)
        for k, step in enumerate(REP_STEPS):
            packed[phase, k, 0] = from_ref[picks[k][0]]
            packed[phase, k, 1] = from_ref[picks[k][1]]
            copy = pltpu.make_async_remote_copy(
                src_ref=packed.at[phase, k], dst_ref=arrived.at[slots, tokens, :],
                send_sem=send.at[phase, k], recv_sem=recv.at[phase, k],
                device_id=(rep_at(rep, step, 1), tp), device_id_type=MESH,
            )
            copy.start()
            bulk[phase].append(copy)
        packed[phase, peers, 0] = from_ref[picks[peers][0]]
        packed[phase, peers, 1] = from_ref[picks[peers][1]]
        copy = pltpu.make_async_copy(packed.at[phase, peers], arrived.at[slots, tokens, :], stay.at[phase])
        copy.start()
        bulk[phase].append(copy)

    own_load.wait()
    send_phase(0, own)

    tp_steps = TP_STEPS + [(0, 0)]
    block = held.shape[2]
    w_loads = []
    for k, step in enumerate(tp_steps):
        at = pl.multiple_of(tp_at(tp, step, 1) * block, block)
        copy = pltpu.make_async_copy(weight.at[:, pl.ds(at, block)], held.at[k], load.at[k])
        copy.start()
        w_loads.append(copy)

    heads = queries.shape[1] // HEAD
    for j in range(heads):
        q3[:, j, :] = queries[:, j * HEAD:(j + 1) * HEAD].astype(jnp.float32)
    pairs = row_count * heads
    q_rows = q3[...].reshape(pairs, HEAD)
    own_now = own_kv[...].astype(jnp.float32)
    own_rows = jnp.broadcast_to(own_now[:, None, :], (row_count, heads, width)).reshape(pairs, width)

    low_col = iota((2 * heads, 1), 0) < heads

    def resident_pair(i, carry):
        a, b = 2 * i, 2 * i + 1
        limits = jnp.where(low_col, res_len[0, a], res_len[0, b])
        peak, total, acc = attend_pair(
            q3[pl.ds(a, 2)].reshape(2 * heads, HEAD), res[a], res[b], limits
        )
        at = pl.ds(pl.multiple_of(i * 2 * heads, 2 * heads), 2 * heads)
        rows3[0, at, :] = jnp.broadcast_to(peak, acc.shape)
        rows3[1, at, :] = jnp.broadcast_to(total, acc.shape)
        rows3[2, at, :] = acc
        return carry

    for k in range(RES_PARTS):
        res_loads[k].wait()
        lax.fori_loop(k * part_rows // 2, (k + 1) * part_rows // 2, resident_pair, 0)
    row_score = jnp.sum(q_rows * own_rows[:, :HEAD], axis=1, keepdims=True) * SCALE
    rows3[2] = combine(rows3[0], rows3[1], rows3[2], row_score, own_rows[:, HEAD:])

    for copy in metas:
        copy.wait_recv()
    codes = meta_all[...].reshape(pairs, HEAD)
    row_of = codes % LEN_UNIT
    lane, sub = iota((pairs, HEAD), 1), iota((pairs, HEAD), 0)
    lanes_rows = HEAD // heads
    for b in range(row_count // lanes_rows):
        hit = (row_of == b * lanes_rows + lane // heads) & (lane % heads == sub % heads)
        selector[:, b * HEAD:(b + 1) * HEAD] = hit.astype(jnp.float32).astype(jnp.bfloat16)
    picked = jnp.dot(selector[...], q_rows.astype(jnp.bfloat16), preferred_element_type=jnp.float32)
    eq3[...] = picked
    picked_kv = jnp.dot(selector[...], own_rows.astype(jnp.bfloat16), preferred_element_type=jnp.float32)
    own_s[...] = jnp.broadcast_to(
        jnp.sum(picked * picked_kv[:, :HEAD], axis=1, keepdims=True) * SCALE, (pairs, HEAD)
    )
    own_v[...] = picked_kv[:, HEAD:]
    own_k[...] = (codes // LEN_UNIT).astype(jnp.int32)
    taken = contract_first(selector[...], jnp.ones((pairs, HEAD), jnp.bfloat16))

    pair.wait_recv()
    send_phase(1, other)

    out_copies = []
    order = [(peers, rep)] + [(k, rep_at(rep, step, -1)) for k, step in enumerate(REP_STEPS)]
    for k, group in order:
        for phase in (0, 1):
            if k == peers:
                bulk[phase][k].wait()
            else:
                bulk[phase][k].wait_recv()
        here = pl.ds(group * CAP, CAP)
        copy = pltpu.make_async_copy(arrived.at[here], arrived_out.at[here], out_sem.at[k])
        copy.start()
        out_copies.append(copy)
        at = pl.ds(pl.multiple_of(group * CAP * heads, CAP * heads), CAP * heads)
        limits = own_k[at, :][:, 0:1]
        peak, total, acc = attend_pair(eq3[at, :], arrived[group * CAP], arrived[group * CAP + 1], limits)
        entry_out[at, :] = combine(peak, total, acc, own_s[at, :], own_v[at, :]).astype(jnp.bfloat16)

    moved = contract_first(selector[...], entry_out[...])
    q3[...] = jnp.where(taken > 0.5, moved, rows3[2]).reshape(row_count, heads, HEAD)
    attention = jnp.concatenate([q3[:, j, :] for j in range(heads)], axis=1).astype(jnp.bfloat16)

    last = len(TP_STEPS)
    scatter = []
    for k, step in enumerate(TP_STEPS):
        w_loads[k].wait()
        staged[k] = jnp.dot(attention, held[k], preferred_element_type=jnp.float32).astype(staged.dtype)
        copy = pltpu.make_async_remote_copy(
            src_ref=staged.at[k], dst_ref=parts.at[k], send_sem=rs_send.at[k], recv_sem=rs_recv.at[k],
            device_id=(rep, tp_at(tp, step, 1)), device_id_type=MESH,
        )
        copy.start()
        scatter.append(copy)
    w_loads[last].wait()
    total = jnp.dot(attention, held[last], preferred_element_type=jnp.float32)
    for k in range(last):
        scatter[k].wait_recv()
        total = total + parts[k].astype(jnp.float32)
    columns = pl.ds(pl.multiple_of(tp * block, block), block)
    attended[:, columns] = total.astype(attended.dtype)
    gather = []
    for k, step in enumerate(TP_STEPS):
        copy = pltpu.make_async_remote_copy(
            src_ref=attended.at[:, columns], dst_ref=attended.at[:, columns], send_sem=ag_send.at[k], recv_sem=ag_recv.at[k],
            device_id=(rep, tp_at(tp, step, 1)), device_id_type=MESH,
        )
        copy.start()
        gather.append(copy)
    pair.wait_send()
    for copy in metas + bulk[0][:peers] + bulk[1][:peers] + scatter:
        copy.wait_send()
    for copy in out_copies + gather:
        copy.wait()


def run_layer(queries, new_token_kv, resident_cache, resident_lengths, new_caches, new_lengths, handoff, out_weight):
    count, _, half, wide = new_caches.shape
    width = wide // 2
    groups, shares = lax.axis_size("rep"), lax.axis_size("tp")
    entries = groups * CAP
    rows, depth = queries.shape
    heads = depth // HEAD
    pairs = rows * heads
    columns = out_weight.shape[1]
    block = columns // shares
    peers, tp_peers = len(REP_STEPS), len(TP_STEPS)
    kind = new_caches.dtype
    dma = pltpu.SemaphoreType.DMA
    vmem = pl.BlockSpec(memory_space=pltpu.VMEM)
    smem = pl.BlockSpec(memory_space=pltpu.SMEM)
    far = pl.BlockSpec(memory_space=pl.ANY)
    return pl.pallas_call(
        layer_kernel,
        out_shape=(
            jax.ShapeDtypeStruct((rows, columns), kind),
            jax.ShapeDtypeStruct((entries, 2 * half, width), kind),
            jax.ShapeDtypeStruct((groups, CAP * heads, HEAD), jnp.int32),
        ),
        in_specs=[smem, smem, smem, vmem, vmem, far, far, far],
        out_specs=(vmem, far, vmem),
        scratch_shapes=[
            pltpu.VMEM((count, half, width), kind),
            pltpu.VMEM((count, half, width), kind),
            pltpu.VMEM((2, groups, CAP, half, width), kind),
            pltpu.VMEM((entries, 2 * half, width), kind),
            pltpu.VMEM(resident_cache.shape, kind),
            pltpu.VMEM((shares, depth, block), kind),
            pltpu.VMEM((groups, CAP * heads, HEAD), jnp.int32),
            pltpu.VMEM((rows, heads, HEAD), jnp.float32),
            pltpu.VMEM((entries * heads, HEAD), jnp.float32),
            pltpu.VMEM((entries * heads, HEAD), jnp.int32),
            pltpu.VMEM((entries * heads, HEAD), jnp.float32),
            pltpu.VMEM((entries * heads, HEAD), jnp.float32),
            pltpu.VMEM((entries * heads, pairs), kind),
            pltpu.VMEM((3, pairs, HEAD), jnp.float32),
            pltpu.VMEM((entries * heads, HEAD), kind),
            pltpu.VMEM((tp_peers, rows, block), kind),
            pltpu.VMEM((tp_peers, rows, block), kind),
            dma, dma, dma, dma((2, peers)), dma((2, peers)), dma((2,)), dma((peers,)), dma((peers,)),
            dma((RES_PARTS,)), dma((peers + 1,)), dma((shares,)),
            dma((tp_peers,)), dma((tp_peers,)), dma((tp_peers,)), dma((tp_peers,)),
        ],
        compiler_params=pltpu.CompilerParams(
            collective_id=0, has_side_effects=True, vmem_limit_bytes=48 * 2**20
        ),
        name="layer",
    )(handoff, new_lengths, resident_lengths, queries, new_token_kv, resident_cache, new_caches, out_weight)


def install_kernel(res_len, own_kv, meta, arrived, resident, updated, buf, own_now, codes, entry, limit, meta_sem, get, put):
    rows, tokens, width = buf.shape
    groups = meta.shape[0]
    heads = meta.shape[1] // CAP
    capacity = arrived.shape[1]
    fetch = pltpu.make_async_copy(meta, codes, meta_sem)
    fetch.start()
    own_now[...] = own_kv[...].astype(jnp.float32)

    def clear(r, carry):
        entry[r] = -1
        limit[r] = res_len[0, jnp.minimum(r, rows - 1)]
        return carry

    lax.fori_loop(0, rows + 1, clear, 0)
    fetch.wait()
    for g in range(groups):
        for s in range(CAP):
            code = codes[g, s * heads, 0]
            row = code % LEN_UNIT
            entry[row] = g * CAP + s
            limit[row] = code // LEN_UNIT

    def get_new(r):
        return pltpu.make_async_copy(arrived.at[entry[r]], buf.at[r, pl.ds(0, capacity), :], get.at[r])

    def get_old(r):
        return pltpu.make_async_copy(resident.at[r], buf.at[r], get.at[r])

    def start(r, carry):
        @pl.when(entry[r] >= 0)
        def _():
            get_new(r).start()

        @pl.when(entry[r] < 0)
        def _():
            get_old(r).start()
        return carry

    lax.fori_loop(0, rows, start, 0)

    def patch(r, carry):
        length = limit[r]
        token = own_now[pl.ds(r, 1), :]

        @pl.when(entry[r] >= 0)
        def _():
            get_new(r).wait()
            at = iota((capacity, width), 0)
            kept = jnp.where(at < length, buf[r, 0:capacity, :].astype(jnp.float32), 0.0)
            buf[r, 0:capacity, :] = jnp.where(at == length, token, kept).astype(buf.dtype)
            at = iota((tokens - capacity, width), 0) + capacity
            buf[r, capacity:tokens, :] = jnp.where(at == length, token, 0.0).astype(buf.dtype)

        @pl.when(entry[r] < 0)
        def _():
            get_old(r).wait()
            first = pl.multiple_of((length // 16) * 16, 16)
            here = buf[r, pl.ds(first, 16), :].astype(jnp.float32)
            at = iota((16, width), 0) + first
            buf[r, pl.ds(first, 16), :] = jnp.where(at == length, token, here).astype(buf.dtype)

        pltpu.make_async_copy(buf.at[r], updated.at[r], put.at[r]).start()
        return carry

    lax.fori_loop(0, rows, patch, 0)

    def finish(r, carry):
        pltpu.make_async_copy(buf.at[r], updated.at[r], put.at[r]).wait()
        return carry

    lax.fori_loop(0, rows, finish, 0)


def install(resident_lengths, new_token_kv, meta, arrived, resident_cache):
    rows, _, width = resident_cache.shape
    dma = pltpu.SemaphoreType.DMA
    vmem = pl.BlockSpec(memory_space=pltpu.VMEM)
    smem = pl.BlockSpec(memory_space=pltpu.SMEM)
    far = pl.BlockSpec(memory_space=pl.ANY)
    return pl.pallas_call(
        install_kernel,
        out_shape=jax.ShapeDtypeStruct(resident_cache.shape, resident_cache.dtype),
        in_specs=[smem, vmem, far, far, far],
        out_specs=far,
        scratch_shapes=[
            pltpu.VMEM(resident_cache.shape, resident_cache.dtype),
            pltpu.VMEM((rows, width), jnp.float32),
            pltpu.SMEM(meta.shape, jnp.int32),
            pltpu.SMEM((rows + 1,), jnp.int32),
            pltpu.SMEM((rows + 1,), jnp.int32),
            dma, dma((rows,)), dma((rows,)),
        ],
        compiler_params=pltpu.CompilerParams(vmem_limit_bytes=48 * 2**20),
        name="install",
    )(resident_lengths, new_token_kv, meta, arrived, resident_cache)


def body(
    queries,
    new_token_kv,
    resident_cache,
    resident_lengths,
    new_caches,
    new_lengths,
    handoff,
    out_weight,
):
    attended, arrived, meta = run_layer(
        queries, new_token_kv, resident_cache, resident_lengths, new_caches, new_lengths, handoff, out_weight
    )
    updated = install(resident_lengths, new_token_kv, meta, arrived, resident_cache)
    return (attended, updated)


def solution(mesh):
    placed = (
        P("rep", "tp"),
        P("rep", "tp"),
        P("rep", None, "tp"),
        P("rep", None),
        P("rep", "tp", None, None),
        P("rep", None),
        P("rep", None, None),
        P("tp", None),
    )
    return jax.shard_map(
        body,
        mesh=mesh,
        in_specs=placed,
        out_specs=(P("rep", None), P("rep", None, "tp")),
        check_vma=False,
    )
```

```python
import functools

import jax
import jax.numpy as jnp
from jax import lax
from jax.experimental import pallas as pl
from jax.experimental.pallas import tpu as pltpu
from jax.sharding import PartitionSpec as P

HEAD = 128
CAP = 2
NEG_FILL = -1e30
SCALE = HEAD ** (-0.5)
MESH = pl.DeviceIdType.MESH
NO_ROW = 32
LEN_UNIT = 64
RES_PARTS = 4
VMEM_BYTES = 63 * 2**20
CHUNKS = 4
PORTIONS = (32, 32, 24, 20, 10)
RES_EARLY = 2

REP_STEPS = [
    (1, 1, 0), (0, 3, 0), (1, 2, 0), (0, 1, 1), (1, 3, 1), (1, 0, 0), (0, 2, 1), (1, 1, 1),
    (0, 3, 1), (1, 2, 1), (0, 1, 0), (1, 3, 0), (1, 0, 1), (0, 2, 0), (0, 0, 1),
]
TP_STEPS = [(h, x) for x in (2, 1, 3, 0) for h in (1, 0) if (h, x) != (0, 0)]
X_STEPS = (2, 1, 3)


def rep_at(rep, step, sign):
    y, z, c = rep // 8, (rep // 2) % 4, rep % 2
    dy, dz, dc = step
    return ((y + dy) % 2) * 8 + ((z + sign * dz + 4) % 4) * 2 + (c + dc) % 2


def tp_at(tp, step, sign):
    h, x = tp // 4, tp % 4
    dh, dx = step
    return ((h + dh) % 2) * 4 + (x + sign * dx + 4) % 4


def iota(shape, dim):
    return lax.broadcasted_iota(jnp.int32, shape, dim)


def contract_last(a, b):
    return lax.dot_general(a, b, (((1,), (1,)), ((), ())), preferred_element_type=jnp.float32)


def contract_first(a, b):
    return lax.dot_general(a, b, (((0,), (0,)), ((), ())), preferred_element_type=jnp.float32)


def attend_pair(query_pair, kv_a, kv_b, limits):
    low = iota(query_pair.shape, 0) < 8
    zero = jnp.zeros_like(query_pair)
    blocks = jnp.concatenate([jnp.where(low, query_pair, zero), jnp.where(low, zero, query_pair)], axis=1)
    keys = jnp.concatenate([kv_a[:, :HEAD], kv_b[:, :HEAD]], axis=1)
    values = jnp.concatenate([kv_a[:, HEAD:], kv_b[:, HEAD:]], axis=1)
    scores = contract_last(blocks.astype(jnp.bfloat16), keys) * SCALE
    allowed = iota(scores.shape, 1) < limits
    peak = jnp.max(jnp.where(allowed, scores, NEG_FILL), axis=1, keepdims=True)
    weights = jnp.where(allowed, jnp.exp(jnp.where(allowed, scores, peak) - peak), 0.0).astype(jnp.bfloat16)
    total = jnp.sum(weights.astype(jnp.float32), axis=1, keepdims=True)
    both = jnp.dot(weights, values, preferred_element_type=jnp.float32)
    return peak, total, jnp.where(low, both[:, :HEAD], both[:, HEAD:])


def combine(peak, total, acc, own_score, own_value):
    top = jnp.maximum(peak, own_score)
    own_weight, factor = jnp.exp(own_score - top), jnp.exp(peak - top)
    return (own_weight * own_value + factor * acc) / (own_weight + factor * total)


def layer_kernel(
    hand, new_len, res_len, queries, own_kv, resident, caches, weight,
    attended, arrived, table,
    meta_send, meta_all, own, theirs, other0, other1, other2, other3, packed, packed2, res, held, q3, query_out, query_in, query_by, acc_by, note_by, part_out, part_in, note_out, note_in,
    selector, rows3, staged, parts, sums,
    own_sem, pair_send, pair_recv, send, recv, stay, meta_s, meta_r, q_s, q_r, p_s, p_r, n_s, n_r, res_sem, load,
    rs_send, rs_recv, swap_send, swap_recv, ag_send, ag_recv,
):
    rep, tp = lax.axis_index("rep"), lax.axis_index("tp")
    parity = tp % 2
    partner = tp + 1 - 2 * parity
    count, half, width = own.shape
    row_count = res.shape[0]
    peers = len(REP_STEPS)
    mine = pl.ds(pl.multiple_of(parity * width, width), width)
    away = pl.ds(pl.multiple_of((1 - parity) * width, width), width)
    own_loads = [
        pltpu.make_async_copy(caches.at[:, 0, :, mine], own, own_sem.at[0]),
        pltpu.make_async_copy(caches.at[:, 0, :, away], theirs, own_sem.at[1]),
    ]
    for copy in own_loads:
        copy.start()
    res_loads = []
    part_rows = row_count // RES_PARTS
    for k in range(RES_PARTS):
        rows = pl.ds(k * part_rows, part_rows)
        copy = pltpu.make_async_copy(resident.at[rows], res.at[rows], res_sem.at[k])
        copy.start()
        res_loads.append(copy)

    barrier = pltpu.get_barrier_semaphore()
    for step in REP_STEPS:
        for to in (tp, partner):
            pl.semaphore_signal(barrier, inc=1, device_id=(rep_at(rep, step, -1), to), device_id_type=MESH)
    for step in TP_STEPS:
        pl.semaphore_signal(barrier, inc=1, device_id=(rep, tp_at(tp, step, -1)), device_id_type=MESH)

    targets = [hand[0, 0, i] for i in range(count)]

    def slot_picks(group):
        seen, first, second = jnp.int32(0), jnp.int32(0), jnp.int32(0)
        for i in range(count):
            hit = targets[i] == group
            first = jnp.where(hit & (seen == 0), i, first)
            second = jnp.where(hit & (seen == 1), i, second)
            seen = seen + hit.astype(jnp.int32)
        return first, second, seen

    def code_of(pick, filled):
        return jnp.where(filled, hand[0, 1, pick] + LEN_UNIT * new_len[0, pick], NO_ROW)

    all_steps = REP_STEPS + [(0, 0, 0)]
    picks = []
    code_lane = iota((1, HEAD), 1)
    for k, step in enumerate(all_steps):
        first, second, seen = slot_picks(rep_at(rep, step, 1))
        picks.append((first, second))
        meta_send[k] = jnp.where(code_lane < HEAD // CAP, code_of(first, seen > 0), code_of(second, seen > 1))
    meta_all[rep] = meta_send[peers]
    pl.semaphore_wait(barrier, 2 * len(REP_STEPS) + len(TP_STEPS))

    metas = []
    for k, step in enumerate(REP_STEPS):
        copy = pltpu.make_async_remote_copy(
            src_ref=meta_send.at[k], dst_ref=meta_all.at[rep], send_sem=meta_s.at[k], recv_sem=meta_r.at[k],
            device_id=(rep_at(rep, step, 1), tp), device_id_type=MESH,
        )
        copy.start()
        metas.append(copy)
    pairs_sent = []
    others = (other0, other1, other2, other3)
    span = half // CHUNKS

    def send_chunk():
        c = len(pairs_sent)
        tokens = pl.ds(c * span, span)
        copy = pltpu.make_async_remote_copy(
            src_ref=caches.at[:, 0, tokens, away], dst_ref=others[c],
            send_sem=pair_send.at[c], recv_sem=pair_recv.at[c], device_id=(rep, partner), device_id_type=MESH,
        )
        copy.start()
        pairs_sent.append(copy)

    slots = pl.ds(rep * CAP, CAP)
    bulk = []
    pieces = [(None, k) for k in range(peers + 1)] + [(c, k) for c in range(CHUNKS) for k in range(peers + 1)]

    def issue(units):
        while units > 0 and len(bulk) < len(pieces):
            c, k = pieces[len(bulk)]
            first, second = picks[k]
            if c is None:
                if k == 0:
                    own_loads[0].wait()
                packed[k, 0] = own[first]
                packed[k, 1] = own[second]
                source, sems = packed.at[k], 0
                tokens = pl.ds(pl.multiple_of(parity * half, half), half)
                units -= CHUNKS
            else:
                if k == 0:
                    pairs_sent[c].wait_recv()
                packed2[c, k, 0] = others[c][first]
                packed2[c, k, 1] = others[c][second]
                source, sems = packed2.at[c, k], c + 1
                tokens = pl.ds(pl.multiple_of((1 - parity) * half + c * span, span), span)
                units -= 1
            if k < peers:
                copy = pltpu.make_async_remote_copy(
                    src_ref=source, dst_ref=arrived.at[slots, tokens, :], send_sem=send.at[sems, k], recv_sem=recv.at[sems, k],
                    device_id=(rep_at(rep, all_steps[k], 1), tp), device_id_type=MESH,
                )
            else:
                copy = pltpu.make_async_copy(source, arrived.at[slots, tokens, :], stay.at[sems])
            copy.start()
            bulk.append(copy)

    send_chunk()
    issue(PORTIONS[0])

    heads = queries.shape[1] // HEAD
    for j in range(heads):
        q3[:, j, :] = queries[:, j * HEAD:(j + 1) * HEAD].astype(jnp.float32)
    pairs = row_count * heads
    tile = CAP * heads
    q_rows = q3[...].reshape(pairs, HEAD)
    own_now = own_kv[...].astype(jnp.float32)
    own_rows = jnp.broadcast_to(own_now[:, None, :], (row_count, heads, width)).reshape(pairs, width)

    for copy in metas:
        copy.wait_recv()
    codes = meta_all[...]
    codes = jnp.stack(
        [jnp.broadcast_to(codes[:, :, at:at + 1], (peers + 1, heads, HEAD)) for at in range(0, HEAD, HEAD // CAP)], axis=1
    ).reshape(pairs, HEAD)
    row_of = codes % LEN_UNIT
    lane, sub = iota((pairs, HEAD), 1), iota((pairs, HEAD), 0)
    lanes_rows = HEAD // heads
    for b in range(row_count // lanes_rows):
        hit = (row_of == b * lanes_rows + lane // heads) & (lane % heads == sub % heads)
        selector[:, b * HEAD:(b + 1) * HEAD] = hit.astype(jnp.float32).astype(jnp.bfloat16)
    picked = jnp.dot(selector[...], q_rows.astype(jnp.bfloat16), preferred_element_type=jnp.float32)
    query_out[...] = picked.astype(jnp.bfloat16).reshape(peers + 1, tile, HEAD)
    query_in[0, rep] = query_out[rep]
    asks = []
    for k, step in enumerate(all_steps):
        group = rep_at(rep, step, 1)
        for w, to in ((0, tp), (1, partner)):
            if k == peers and w == 0:
                continue
            copy = pltpu.make_async_remote_copy(
                src_ref=query_out.at[group], dst_ref=query_in.at[w, rep], send_sem=q_s.at[w, k], recv_sem=q_r.at[w, k],
                device_id=(group, to), device_id_type=MESH,
            )
            copy.start()
            asks.append(copy)
    send_chunk()
    send_chunk()
    issue(PORTIONS[1])

    low_col = iota((tile, 1), 0) < heads

    def resident_pair(i, carry):
        a, b = 2 * i, 2 * i + 1
        limits = jnp.where(low_col, res_len[0, a], res_len[0, b])
        peak, total, acc = attend_pair(q3[pl.ds(a, 2)].reshape(tile, HEAD), res[a], res[b], limits)
        at = pl.ds(pl.multiple_of(i * tile, tile), tile)
        rows3[0, at, :] = jnp.broadcast_to(peak, acc.shape)
        rows3[1, at, :] = jnp.broadcast_to(total, acc.shape)
        rows3[2, at, :] = acc
        return carry

    def resident_part(k):
        res_loads[k].wait()
        lax.fori_loop(k * part_rows // 2, (k + 1) * part_rows // 2, resident_pair, 0)

    for k in range(RES_EARLY):
        resident_part(k)

    for copy in asks:
        copy.wait_recv()
    own_loads[1].wait()
    query_by[...] = query_in[...].astype(jnp.float32).reshape(query_by.shape)

    for i in range(count):
        at = targets[i] * CAP + sum([(targets[n] == targets[i]).astype(jnp.int32) for n in range(i)], jnp.int32(0))
        asked = jnp.concatenate([query_by[0, at], query_by[1, at]], axis=0)
        peak, total, acc = attend_pair(asked, own[i], theirs[i], new_len[0, i] - half * parity)
        acc_by[i] = acc
        peak, total = jnp.broadcast_to(peak, acc.shape), jnp.broadcast_to(total, acc.shape)
        note_by[i] = jnp.where(iota(acc.shape, 1) % 2 == 0, peak, total)
    note_lane, note_sub = iota((heads, HEAD), 1), iota((heads, HEAD), 0)
    answers = []
    for k, step in enumerate(all_steps):
        first, second = picks[k]
        group = rep_at(rep, step, 1)
        for w, to in ((0, tp), (1, partner)):
            of = slice(w * heads, (w + 1) * heads)
            both = jnp.concatenate([acc_by[first][of], acc_by[second][of]], axis=0).astype(part_out.dtype)
            note = jnp.where(note_lane % 4 < 2, note_by[first][of], note_by[second][of])
            note = jnp.sum(jnp.where(note_lane // 4 == note_sub, note, 0.0), axis=0, keepdims=True)
            if k == peers and w == 0:
                part_in[0, rep] = both
                note_in[0, rep] = note
                continue
            part_out[w, k] = both
            note_out[w, k] = note
            for source, target, out_sem, in_sem in ((part_out, part_in, p_s, p_r), (note_out, note_in, n_s, n_r)):
                copy = pltpu.make_async_remote_copy(
                    src_ref=source.at[w, k], dst_ref=target.at[w, rep], send_sem=out_sem.at[w, k], recv_sem=in_sem.at[w, k],
                    device_id=(group, to), device_id_type=MESH,
                )
                copy.start()
                answers.append(copy)
    send_chunk()
    issue(PORTIONS[2])
    here = tp % 4
    block = held.shape[2]
    w_loads = []
    for k, step in enumerate(X_STEPS + (0,)):
        at = pl.multiple_of(((here + step) % 4) * block, block)
        copy = pltpu.make_async_copy(weight.at[:, pl.ds(at, block)], held.at[k], load.at[k])
        copy.start()
        w_loads.append(copy)

    for k in range(RES_EARLY, RES_PARTS):
        resident_part(k)
    row_score = jnp.sum(q_rows * own_rows[:, :HEAD], axis=1, keepdims=True) * SCALE
    rows3[2] = combine(rows3[0], rows3[1], rows3[2], row_score, own_rows[:, HEAD:])
    picked_kv = jnp.dot(selector[...], own_rows.astype(jnp.bfloat16), preferred_element_type=jnp.float32)
    entry_score = jnp.sum(picked * picked_kv[:, :HEAD], axis=1, keepdims=True) * SCALE
    taken = contract_first(selector[...], jnp.ones((pairs, HEAD), jnp.bfloat16))
    entry_of = (sub // heads + 1).astype(jnp.float32)
    notes = jnp.where(lane == 0, entry_of, jnp.where(lane == 1, (codes // LEN_UNIT).astype(jnp.float32), 0.0))
    table[...] = contract_first(notes.astype(jnp.bfloat16), selector[...])[0:8, :].astype(jnp.int32)

    for copy in answers:
        copy.wait_recv()
    peaks, totals, accs = [], [], []
    cell, cell_sub = iota((peers + 1, heads, HEAD), 2), iota((peers + 1, heads, HEAD), 1)
    for w in range(CAP):
        accs.append(part_in[w].astype(jnp.float32).reshape(pairs, HEAD))
        note = jnp.broadcast_to(note_in[w], cell.shape)

        def column(at):
            found = jnp.sum(jnp.where(cell == 4 * cell_sub + at, note, 0.0), axis=2, keepdims=True)
            return jnp.broadcast_to(found, cell.shape)

        peaks.append(jnp.stack([column(0), column(2)], axis=1).reshape(pairs, HEAD))
        totals.append(jnp.stack([column(1), column(3)], axis=1).reshape(pairs, HEAD))
    top = jnp.maximum(jnp.maximum(peaks[0], peaks[1]), entry_score)
    own_weight = jnp.exp(entry_score - top)
    factors = [jnp.exp(peak - top) for peak in peaks]
    above = own_weight * picked_kv[:, HEAD:] + factors[0] * accs[0] + factors[1] * accs[1]
    below = own_weight + factors[0] * totals[0] + factors[1] * totals[1]
    moved = contract_first(selector[...], (above / below).astype(jnp.bfloat16))
    q3[...] = jnp.where(taken > 0.5, moved, rows3[2]).reshape(row_count, heads, HEAD)
    attention = jnp.concatenate([q3[:, j, :] for j in range(heads)], axis=1).astype(jnp.bfloat16)

    def x_at(step):
        return (tp // 4) * 4 + (here + step) % 4

    last = len(X_STEPS)
    scatter = []
    for k, step in enumerate(X_STEPS):
        w_loads[k].wait()
        staged[k] = jnp.dot(attention, held[k], preferred_element_type=jnp.float32).astype(staged.dtype)
        copy = pltpu.make_async_remote_copy(
            src_ref=staged.at[k], dst_ref=parts.at[k], send_sem=rs_send.at[k], recv_sem=rs_recv.at[k],
            device_id=(rep, x_at(step)), device_id_type=MESH,
        )
        copy.start()
        scatter.append(copy)
    issue(PORTIONS[3])
    w_loads[last].wait()
    total = jnp.dot(attention, held[last], preferred_element_type=jnp.float32)
    for k in range(last):
        scatter[k].wait_recv()
        total = total + parts[k].astype(jnp.float32)
    sums[0] = total.astype(sums.dtype)
    swap = pltpu.make_async_remote_copy(
        src_ref=sums.at[0], dst_ref=sums.at[1], send_sem=swap_send, recv_sem=swap_recv,
        device_id=(rep, (tp + 4) % 8), device_id_type=MESH,
    )
    swap.start()
    issue(PORTIONS[4])
    swap.wait_recv()
    columns = pl.ds(pl.multiple_of(here * block, block), block)
    attended[:, columns] = (sums[0].astype(jnp.float32) + sums[1].astype(jnp.float32)).astype(attended.dtype)
    gather = []
    for k, step in enumerate(X_STEPS):
        copy = pltpu.make_async_remote_copy(
            src_ref=attended.at[:, columns], dst_ref=attended.at[:, columns], send_sem=ag_send.at[k], recv_sem=ag_recv.at[k],
            device_id=(rep, x_at(step)), device_id_type=MESH,
        )
        copy.start()
        gather.append(copy)
    issue(len(pieces) * CHUNKS)
    swap.wait_send()
    for copy in pairs_sent:
        copy.wait_send()
    for copy in metas + asks + answers + scatter:
        copy.wait_send()
    for copy in gather + bulk:
        copy.wait()


def run_layer(queries, new_token_kv, resident_cache, resident_lengths, new_caches, new_lengths, handoff, out_weight):
    count, _, half, wide = new_caches.shape
    width = wide // 2
    groups = lax.axis_size("rep")
    entries = groups * CAP
    rows, depth = queries.shape
    heads = depth // HEAD
    tile = CAP * heads
    pairs = rows * heads
    columns = out_weight.shape[1]
    wide_x = len(X_STEPS) + 1
    block = columns // wide_x
    peers, x_peers = len(REP_STEPS), len(X_STEPS)
    kind = new_caches.dtype
    dma = pltpu.SemaphoreType.DMA
    vmem = pl.BlockSpec(memory_space=pltpu.VMEM)
    smem = pl.BlockSpec(memory_space=pltpu.SMEM)
    far = pl.BlockSpec(memory_space=pl.ANY)
    f32 = jnp.float32
    return pl.pallas_call(
        layer_kernel,
        out_shape=(
            jax.ShapeDtypeStruct((rows, columns), kind),
            jax.ShapeDtypeStruct((entries, 2 * half, width), kind),
            jax.ShapeDtypeStruct((8, pairs), jnp.int32),
        ),
        in_specs=[smem, smem, smem, vmem, vmem, far, far, far],
        out_specs=(vmem, far, vmem),
        scratch_shapes=[
            pltpu.VMEM((groups, 1, HEAD), jnp.int32),
            pltpu.VMEM((groups, 1, HEAD), jnp.int32),
            pltpu.VMEM((count, half, width), kind),
            pltpu.VMEM((count, half, width), kind),
            *[pltpu.VMEM((count, half // CHUNKS, width), kind)] * CHUNKS,
            pltpu.VMEM((groups, CAP, half, width), kind),
            pltpu.VMEM((CHUNKS, groups, CAP, half // CHUNKS, width), kind),
            pltpu.VMEM(resident_cache.shape, kind),
            pltpu.VMEM((wide_x, depth, block), kind),
            pltpu.VMEM((rows, heads, HEAD), f32),
            pltpu.VMEM((groups, tile, HEAD), kind),
            pltpu.VMEM((2, groups, tile, HEAD), kind),
            pltpu.VMEM((2, entries, heads, HEAD), f32),
            pltpu.VMEM((count, tile, HEAD), f32),
            pltpu.VMEM((count, tile, HEAD), f32),
            pltpu.VMEM((2, groups, tile, HEAD), kind),
            pltpu.VMEM((2, groups, tile, HEAD), kind),
            pltpu.VMEM((2, groups, 1, HEAD), f32),
            pltpu.VMEM((2, groups, 1, HEAD), f32),
            pltpu.VMEM((entries * heads, pairs), kind),
            pltpu.VMEM((3, pairs, HEAD), f32),
            pltpu.VMEM((x_peers, rows, block), kind),
            pltpu.VMEM((x_peers, rows, block), kind),
            pltpu.VMEM((2, rows, block), kind),
            dma((2,)), dma((CHUNKS,)), dma((CHUNKS,)), dma((CHUNKS + 1, peers)), dma((CHUNKS + 1, peers)), dma((CHUNKS + 1,)),
            dma((peers,)), dma((peers,)),
            dma((2, groups)), dma((2, groups)), dma((2, groups)), dma((2, groups)), dma((2, groups)), dma((2, groups)), dma((RES_PARTS,)), dma((wide_x,)),
            dma((x_peers,)), dma((x_peers,)), dma, dma, dma((x_peers,)), dma((x_peers,)),
        ],
        compiler_params=pltpu.CompilerParams(
            collective_id=0, has_side_effects=True, vmem_limit_bytes=VMEM_BYTES
        ),
        name="layer",
    )(jnp.swapaxes(handoff, 1, 2), new_lengths, resident_lengths, queries, new_token_kv, resident_cache, new_caches, out_weight)


def install_kernel(res_len, own_kv, table, arrived, resident, updated, buf, own_now, notes, note_sem, get, put):
    rows, tokens, width = buf.shape
    heads = table.shape[1] // rows
    capacity = arrived.shape[1]
    step = 16
    fetch = pltpu.make_async_copy(table, notes, note_sem)
    fetch.start()
    own_now[...] = own_kv[...].astype(jnp.float32)
    fetch.wait()

    def entry(r):
        return notes[0, r * heads] - 1

    def get_new(r):
        return pltpu.make_async_copy(arrived.at[entry(r)], buf.at[r, pl.ds(0, capacity), :], get.at[r])

    def get_old(r):
        return pltpu.make_async_copy(resident.at[r], buf.at[r], get.at[r])

    def start(r, carry):
        @pl.when(entry(r) >= 0)
        def _():
            get_new(r).start()

        @pl.when(entry(r) < 0)
        def _():
            get_old(r).start()
        return carry

    lax.fori_loop(0, rows, start, 0)
    at = iota((step, width), 0)

    def patch(r, carry):
        token = own_now[pl.ds(r, 1), :]
        new = entry(r) >= 0
        length = jnp.where(new, notes[1, r * heads], res_len[0, r])
        block = length // step
        here = pl.ds(pl.multiple_of(block * step, step), step)

        @pl.when(new)
        def _():
            get_new(r).wait()
            kept = jnp.where(at < length - block * step, buf[r, here, :].astype(jnp.float32), 0.0)
            buf[r, here, :] = jnp.where(at == length - block * step, token, kept).astype(buf.dtype)

            def clear(i, carry):
                buf[r, pl.ds(pl.multiple_of(i * step, step), step), :] = jnp.zeros((step, width), buf.dtype)
                return carry

            lax.fori_loop(block + 1, tokens // step, clear, 0)

        @pl.when(jnp.logical_not(new))
        def _():
            get_old(r).wait()
            kept = buf[r, here, :].astype(jnp.float32)
            buf[r, here, :] = jnp.where(at == length - block * step, token, kept).astype(buf.dtype)

        pltpu.make_async_copy(buf.at[r], updated.at[r], put.at[r]).start()
        return carry

    lax.fori_loop(0, rows, patch, 0)

    def finish(r, carry):
        pltpu.make_async_copy(buf.at[r], updated.at[r], put.at[r]).wait()
        return carry

    lax.fori_loop(0, rows, finish, 0)


def install(resident_lengths, new_token_kv, table, arrived, resident_cache):
    rows, _, width = resident_cache.shape
    dma = pltpu.SemaphoreType.DMA
    vmem = pl.BlockSpec(memory_space=pltpu.VMEM)
    smem = pl.BlockSpec(memory_space=pltpu.SMEM)
    far = pl.BlockSpec(memory_space=pl.ANY)
    return pl.pallas_call(
        install_kernel,
        out_shape=jax.ShapeDtypeStruct(resident_cache.shape, resident_cache.dtype),
        in_specs=[smem, vmem, far, far, far],
        out_specs=far,
        scratch_shapes=[
            pltpu.VMEM(resident_cache.shape, resident_cache.dtype),
            pltpu.VMEM((rows, width), jnp.float32),
            pltpu.SMEM(table.shape, jnp.int32),
            dma, dma((rows,)), dma((rows,)),
        ],
        compiler_params=pltpu.CompilerParams(vmem_limit_bytes=VMEM_BYTES),
        name="install",
    )(resident_lengths, new_token_kv, table, arrived, resident_cache)


def body(
    queries,
    new_token_kv,
    resident_cache,
    resident_lengths,
    new_caches,
    new_lengths,
    handoff,
    out_weight,
):
    attended, arrived, table = run_layer(
        queries, new_token_kv, resident_cache, resident_lengths, new_caches, new_lengths, handoff, out_weight
    )
    updated = install(resident_lengths, new_token_kv, table, arrived, resident_cache)
    return (attended, updated)


def solution(mesh):
    placed = (
        P("rep", "tp"),
        P("rep", "tp"),
        P("rep", None, "tp"),
        P("rep", None),
        P("rep", "tp", None, None),
        P("rep", None),
        P("rep", None, None),
        P("tp", None),
    )
    return jax.shard_map(
        body,
        mesh=mesh,
        in_specs=placed,
        out_specs=(P("rep", None), P("rep", None, "tp")),
        check_vma=False,
    )
```

```python
import functools

import jax
import jax.numpy as jnp
from jax import lax
from jax.experimental import pallas as pl
from jax.experimental.pallas import tpu as pltpu
from jax.sharding import PartitionSpec as P

HEAD = 128
CAP = 2
NEG_FILL = -1e30
SCALE = HEAD ** (-0.5)
MESH = pl.DeviceIdType.MESH
NO_ROW = 32
LEN_UNIT = 64
RES_PARTS = 4
VMEM_BYTES = 63 * 2**20
CHUNKS = 4
PORTIONS = (28, 32, 24, 20, 24)
RES_EARLY = 2
SPLITS = 2

REP_STEPS = [
    (1, 1, 0), (0, 3, 0), (1, 2, 0), (0, 1, 1), (1, 3, 1), (1, 0, 0), (0, 2, 1), (1, 1, 1),
    (0, 3, 1), (1, 2, 1), (0, 1, 0), (1, 3, 0), (1, 0, 1), (0, 2, 0), (0, 0, 1),
]
TP_STEPS = [(h, x) for x in (2, 1, 3, 0) for h in (1, 0) if (h, x) != (0, 0)]
X_STEPS = (2, 1, 3)


def rep_at(rep, step, sign):
    y, z, c = rep // 8, (rep // 2) % 4, rep % 2
    dy, dz, dc = step
    return ((y + dy) % 2) * 8 + ((z + sign * dz + 4) % 4) * 2 + (c + dc) % 2


def tp_at(tp, step, sign):
    h, x = tp // 4, tp % 4
    dh, dx = step
    return ((h + dh) % 2) * 4 + (x + sign * dx + 4) % 4


def iota(shape, dim):
    return lax.broadcasted_iota(jnp.int32, shape, dim)


def contract_last(a, b):
    return lax.dot_general(a, b, (((1,), (1,)), ((), ())), preferred_element_type=jnp.float32)


def contract_first(a, b):
    return lax.dot_general(a, b, (((0,), (0,)), ((), ())), preferred_element_type=jnp.float32)


def attend_pair(query_pair, kv_a, kv_b, limits):
    low = iota(query_pair.shape, 0) < 8
    zero = jnp.zeros_like(query_pair)
    blocks = jnp.concatenate([jnp.where(low, query_pair, zero), jnp.where(low, zero, query_pair)], axis=1)
    keys = jnp.concatenate([kv_a[:, :HEAD], kv_b[:, :HEAD]], axis=1)
    values = jnp.concatenate([kv_a[:, HEAD:], kv_b[:, HEAD:]], axis=1)
    scores = contract_last(blocks.astype(jnp.bfloat16), keys) * SCALE
    allowed = iota(scores.shape, 1) < limits
    peak = jnp.max(jnp.where(allowed, scores, NEG_FILL), axis=1, keepdims=True)
    weights = jnp.where(allowed, jnp.exp(jnp.where(allowed, scores, peak) - peak), 0.0).astype(jnp.bfloat16)
    total = jnp.sum(weights.astype(jnp.float32), axis=1, keepdims=True)
    both = jnp.dot(weights, values, preferred_element_type=jnp.float32)
    return peak, total, jnp.where(low, both[:, :HEAD], both[:, HEAD:])


def combine(peak, total, acc, own_score, own_value):
    top = jnp.maximum(peak, own_score)
    own_weight, factor = jnp.exp(own_score - top), jnp.exp(peak - top)
    return (own_weight * own_value + factor * acc) / (own_weight + factor * total)


def layer_kernel(
    hand_far, new_len_far, res_len_far, queries_far, own_kv_far, resident, caches, weight,
    attended_far, arrived, table_far,
    attended, table, hand, new_len, res_len, queries, own_kv,
    meta_send, meta_all, own, theirs, other0, other1, other2, other3, packed, packed2, res, held, q3, query_out, query_in, query_by, acc_by, note_by, part_out, part_in, note_out, note_in,
    selector, rows3, staged, parts, sums,
    own_sem, pair_send, pair_recv, send, recv, stay, meta_s, meta_r, q_s, q_r, p_s, p_r, n_s, n_r, res_sem, load,
    rs_send, rs_recv, swap_send, swap_recv, ag_send, ag_recv, small_sem, result_sem,
):
    rep, tp = lax.axis_index("rep"), lax.axis_index("tp")
    parity = tp % 2
    partner = tp + 1 - 2 * parity
    count, half, width = own.shape
    row_count = res.shape[0]
    peers = len(REP_STEPS)
    smalls = []
    for k, (source, target) in enumerate(
        ((hand_far, hand), (new_len_far, new_len), (queries_far, queries), (own_kv_far, own_kv), (res_len_far, res_len))
    ):
        copy = pltpu.make_async_copy(source, target, small_sem.at[k])
        copy.start()
        smalls.append(copy)
    mine = pl.ds(pl.multiple_of(parity * width, width), width)
    away = pl.ds(pl.multiple_of((1 - parity) * width, width), width)
    own_loads = [
        pltpu.make_async_copy(caches.at[:, 0, :, mine], own, own_sem.at[0]),
        pltpu.make_async_copy(caches.at[:, 0, :, away], theirs, own_sem.at[1]),
    ]
    for copy in own_loads:
        copy.start()
    res_loads = []
    part_rows = row_count // RES_PARTS
    for k in range(RES_PARTS):
        rows = pl.ds(k * part_rows, part_rows)
        copy = pltpu.make_async_copy(resident.at[rows], res.at[rows], res_sem.at[k])
        copy.start()
        res_loads.append(copy)

    barrier = pltpu.get_barrier_semaphore()
    for step in REP_STEPS:
        for to in (tp, partner):
            pl.semaphore_signal(barrier, inc=1, device_id=(rep_at(rep, step, -1), to), device_id_type=MESH)
    for step in TP_STEPS:
        pl.semaphore_signal(barrier, inc=1, device_id=(rep, tp_at(tp, step, -1)), device_id_type=MESH)

    for copy in smalls[:2]:
        copy.wait()
    targets = [hand[0, 0, i] for i in range(count)]

    def slot_picks(group):
        seen, first, second = jnp.int32(0), jnp.int32(0), jnp.int32(0)
        for i in range(count):
            hit = targets[i] == group
            first = jnp.where(hit & (seen == 0), i, first)
            second = jnp.where(hit & (seen == 1), i, second)
            seen = seen + hit.astype(jnp.int32)
        return first, second, seen

    def code_of(pick, filled):
        return jnp.where(filled, hand[0, 1, pick] + LEN_UNIT * new_len[0, pick], NO_ROW)

    all_steps = REP_STEPS + [(0, 0, 0)]
    picks = []
    code_lane = iota((1, HEAD), 1)
    for k, step in enumerate(all_steps):
        first, second, seen = slot_picks(rep_at(rep, step, 1))
        picks.append((first, second))
        meta_send[k] = jnp.where(code_lane < HEAD // CAP, code_of(first, seen > 0), code_of(second, seen > 1))
    meta_all[rep] = meta_send[peers]
    pl.semaphore_wait(barrier, 2 * len(REP_STEPS) + len(TP_STEPS))

    metas = []
    for k, step in enumerate(REP_STEPS):
        copy = pltpu.make_async_remote_copy(
            src_ref=meta_send.at[k], dst_ref=meta_all.at[rep], send_sem=meta_s.at[k], recv_sem=meta_r.at[k],
            device_id=(rep_at(rep, step, 1), tp), device_id_type=MESH,
        )
        copy.start()
        metas.append(copy)
    pairs_sent = []
    others = (other0, other1, other2, other3)
    span = half // CHUNKS

    def send_chunk():
        c = len(pairs_sent)
        tokens = pl.ds(c * span, span)
        copy = pltpu.make_async_remote_copy(
            src_ref=caches.at[:, 0, tokens, away], dst_ref=others[c],
            send_sem=pair_send.at[c], recv_sem=pair_recv.at[c], device_id=(rep, partner), device_id_type=MESH,
        )
        copy.start()
        pairs_sent.append(copy)

    slots = pl.ds(rep * CAP, CAP)
    bulk = []
    pieces = [(None, k) for k in range(peers + 1)] + [(c, k) for c in range(CHUNKS) for k in range(peers + 1)]

    def issue(units):
        while units > 0 and len(bulk) < len(pieces):
            c, k = pieces[len(bulk)]
            first, second = picks[k]
            if c is None:
                if k == 0:
                    own_loads[0].wait()
                packed[k, 0] = own[first]
                packed[k, 1] = own[second]
                source, sems = packed.at[k], 0
                tokens = pl.ds(pl.multiple_of(parity * half, half), half)
                units -= CHUNKS
            else:
                if k == 0:
                    pairs_sent[c].wait_recv()
                packed2[c, k, 0] = others[c][first]
                packed2[c, k, 1] = others[c][second]
                source, sems = packed2.at[c, k], c + 1
                tokens = pl.ds(pl.multiple_of((1 - parity) * half + c * span, span), span)
                units -= 1
            if k < peers:
                copy = pltpu.make_async_remote_copy(
                    src_ref=source, dst_ref=arrived.at[slots, tokens, :], send_sem=send.at[sems, k], recv_sem=recv.at[sems, k],
                    device_id=(rep_at(rep, all_steps[k], 1), tp), device_id_type=MESH,
                )
            else:
                copy = pltpu.make_async_copy(source, arrived.at[slots, tokens, :], stay.at[sems])
            copy.start()
            bulk.append(copy)

    send_chunk()
    issue(PORTIONS[0])

    for copy in smalls[2:]:
        copy.wait()
    heads = queries.shape[1] // HEAD
    for j in range(heads):
        q3[:, j, :] = queries[:, j * HEAD:(j + 1) * HEAD].astype(jnp.float32)
    pairs = row_count * heads
    tile = CAP * heads
    q_rows = q3[...].reshape(pairs, HEAD)
    own_now = own_kv[...].astype(jnp.float32)
    own_rows = jnp.broadcast_to(own_now[:, None, :], (row_count, heads, width)).reshape(pairs, width)

    for copy in metas:
        copy.wait_recv()
    codes = meta_all[...]
    codes = jnp.stack(
        [jnp.broadcast_to(codes[:, :, at:at + 1], (peers + 1, heads, HEAD)) for at in range(0, HEAD, HEAD // CAP)], axis=1
    ).reshape(pairs, HEAD)
    row_of = codes % LEN_UNIT
    lane, sub = iota((pairs, HEAD), 1), iota((pairs, HEAD), 0)
    lanes_rows = HEAD // heads
    for b in range(row_count // lanes_rows):
        hit = (row_of == b * lanes_rows + lane // heads) & (lane % heads == sub % heads)
        selector[:, b * HEAD:(b + 1) * HEAD] = hit.astype(jnp.float32).astype(jnp.bfloat16)
    picked = jnp.dot(selector[...], q_rows.astype(jnp.bfloat16), preferred_element_type=jnp.float32)
    query_out[...] = picked.astype(jnp.bfloat16).reshape(peers + 1, tile, HEAD)
    query_in[0, rep] = query_out[rep]
    asks = []
    for k, step in enumerate(all_steps):
        group = rep_at(rep, step, 1)
        for w, to in ((0, tp), (1, partner)):
            if k == peers and w == 0:
                continue
            copy = pltpu.make_async_remote_copy(
                src_ref=query_out.at[group], dst_ref=query_in.at[w, rep], send_sem=q_s.at[w, k], recv_sem=q_r.at[w, k],
                device_id=(group, to), device_id_type=MESH,
            )
            copy.start()
            asks.append(copy)
    send_chunk()
    send_chunk()
    issue(PORTIONS[1])

    low_col = iota((tile, 1), 0) < heads

    def resident_pair(i, carry):
        a, b = 2 * i, 2 * i + 1
        limits = jnp.where(low_col, res_len[0, a], res_len[0, b])
        peak, total, acc = attend_pair(q3[pl.ds(a, 2)].reshape(tile, HEAD), res[a], res[b], limits)
        at = pl.ds(pl.multiple_of(i * tile, tile), tile)
        rows3[0, at, :] = jnp.broadcast_to(peak, acc.shape)
        rows3[1, at, :] = jnp.broadcast_to(total, acc.shape)
        rows3[2, at, :] = acc
        return carry

    def resident_part(k):
        res_loads[k].wait()
        lax.fori_loop(k * part_rows // 2, (k + 1) * part_rows // 2, resident_pair, 0)

    for k in range(RES_EARLY):
        resident_part(k)

    for copy in asks:
        copy.wait_recv()
    own_loads[1].wait()
    query_by[...] = query_in[...].astype(jnp.float32).reshape(query_by.shape)

    for i in range(count):
        at = targets[i] * CAP + sum([(targets[n] == targets[i]).astype(jnp.int32) for n in range(i)], jnp.int32(0))
        asked = jnp.concatenate([query_by[0, at], query_by[1, at]], axis=0)
        peak, total, acc = attend_pair(asked, own[i], theirs[i], new_len[0, i] - half * parity)
        acc_by[i] = acc
        peak, total = jnp.broadcast_to(peak, acc.shape), jnp.broadcast_to(total, acc.shape)
        note_by[i] = jnp.where(iota(acc.shape, 1) % 2 == 0, peak, total)
    note_lane, note_sub = iota((heads, HEAD), 1), iota((heads, HEAD), 0)
    answers = []
    for k, step in enumerate(all_steps):
        first, second = picks[k]
        group = rep_at(rep, step, 1)
        for w, to in ((0, tp), (1, partner)):
            of = slice(w * heads, (w + 1) * heads)
            both = jnp.concatenate([acc_by[first][of], acc_by[second][of]], axis=0).astype(part_out.dtype)
            note = jnp.where(note_lane % 4 < 2, note_by[first][of], note_by[second][of])
            note = jnp.sum(jnp.where(note_lane // 4 == note_sub, note, 0.0), axis=0, keepdims=True)
            if k == peers and w == 0:
                part_in[0, rep] = both
                note_in[0, rep] = note
                continue
            part_out[w, k] = both
            note_out[w, k] = note
            for source, target, out_sem, in_sem in ((part_out, part_in, p_s, p_r), (note_out, note_in, n_s, n_r)):
                copy = pltpu.make_async_remote_copy(
                    src_ref=source.at[w, k], dst_ref=target.at[w, rep], send_sem=out_sem.at[w, k], recv_sem=in_sem.at[w, k],
                    device_id=(group, to), device_id_type=MESH,
                )
                copy.start()
                answers.append(copy)
    send_chunk()
    issue(PORTIONS[2])
    here = tp % 4
    block = held.shape[2]
    w_loads = []
    for k, step in enumerate(X_STEPS + (0,)):
        at = pl.multiple_of(((here + step) % 4) * block, block)
        copy = pltpu.make_async_copy(weight.at[:, pl.ds(at, block)], held.at[k], load.at[k])
        copy.start()
        w_loads.append(copy)

    for k in range(RES_EARLY, RES_PARTS):
        resident_part(k)
    row_score = jnp.sum(q_rows * own_rows[:, :HEAD], axis=1, keepdims=True) * SCALE
    rows3[2] = combine(rows3[0], rows3[1], rows3[2], row_score, own_rows[:, HEAD:])
    picked_kv = jnp.dot(selector[...], own_rows.astype(jnp.bfloat16), preferred_element_type=jnp.float32)
    entry_score = jnp.sum(picked * picked_kv[:, :HEAD], axis=1, keepdims=True) * SCALE
    taken = contract_first(selector[...], jnp.ones((pairs, HEAD), jnp.bfloat16))
    entry_of = (sub // heads + 1).astype(jnp.float32)
    notes = jnp.where(lane == 0, entry_of, jnp.where(lane == 1, (codes // LEN_UNIT).astype(jnp.float32), 0.0))
    table[...] = contract_first(notes.astype(jnp.bfloat16), selector[...])[0:8, :].astype(jnp.int32)
    results = [
        pltpu.make_async_copy(table, table_far, result_sem.at[0]),
        pltpu.make_async_copy(attended, attended_far, result_sem.at[1]),
    ]
    results[0].start()

    for copy in answers:
        copy.wait_recv()
    peaks, totals, accs = [], [], []
    cell, cell_sub = iota((peers + 1, heads, HEAD), 2), iota((peers + 1, heads, HEAD), 1)
    for w in range(CAP):
        accs.append(part_in[w].astype(jnp.float32).reshape(pairs, HEAD))
        note = jnp.broadcast_to(note_in[w], cell.shape)

        def column(at):
            found = jnp.sum(jnp.where(cell == 4 * cell_sub + at, note, 0.0), axis=2, keepdims=True)
            return jnp.broadcast_to(found, cell.shape)

        peaks.append(jnp.stack([column(0), column(2)], axis=1).reshape(pairs, HEAD))
        totals.append(jnp.stack([column(1), column(3)], axis=1).reshape(pairs, HEAD))
    top = jnp.maximum(jnp.maximum(peaks[0], peaks[1]), entry_score)
    own_weight = jnp.exp(entry_score - top)
    factors = [jnp.exp(peak - top) for peak in peaks]
    above = own_weight * picked_kv[:, HEAD:] + factors[0] * accs[0] + factors[1] * accs[1]
    below = own_weight + factors[0] * totals[0] + factors[1] * totals[1]
    moved = contract_first(selector[...], (above / below).astype(jnp.bfloat16))
    q3[...] = jnp.where(taken > 0.5, moved, rows3[2]).reshape(row_count, heads, HEAD)
    attention = jnp.concatenate([q3[:, j, :] for j in range(heads)], axis=1).astype(jnp.bfloat16)

    def x_at(step):
        return (tp // 4) * 4 + (here + step) % 4

    last = len(X_STEPS)
    part_width = block // SPLITS

    def share(k, split):
        at = slice(split * part_width, (split + 1) * part_width)
        return jnp.dot(attention, held[k, :, at], preferred_element_type=jnp.float32)

    scatter = []
    for split in range(SPLITS):
        for k, step in enumerate(X_STEPS):
            if split == 0:
                w_loads[k].wait()
            staged[split, k] = share(k, split).astype(staged.dtype)
            copy = pltpu.make_async_remote_copy(
                src_ref=staged.at[split, k], dst_ref=parts.at[split, k],
                send_sem=rs_send.at[split, k], recv_sem=rs_recv.at[split, k],
                device_id=(rep, x_at(step)), device_id_type=MESH,
            )
            copy.start()
            scatter.append(copy)
    issue(PORTIONS[3])
    w_loads[last].wait()
    swaps = []
    for split in range(SPLITS):
        total = share(last, split)
        for k in range(last):
            scatter[split * last + k].wait_recv()
            total = total + parts[split, k].astype(jnp.float32)
        sums[split, 0] = total.astype(sums.dtype)
        copy = pltpu.make_async_remote_copy(
            src_ref=sums.at[split, 0], dst_ref=sums.at[split, 1], send_sem=swap_send.at[split], recv_sem=swap_recv.at[split],
            device_id=(rep, (tp + 4) % 8), device_id_type=MESH,
        )
        copy.start()
        swaps.append(copy)
    issue(PORTIONS[4])
    gather = []
    for split in range(SPLITS):
        swaps[split].wait_recv()
        columns = pl.ds(pl.multiple_of(here * block + split * part_width, part_width), part_width)
        both = sums[split, 0].astype(jnp.float32) + sums[split, 1].astype(jnp.float32)
        attended[:, columns] = both.astype(attended.dtype)
        for k, step in enumerate(X_STEPS):
            copy = pltpu.make_async_remote_copy(
                src_ref=attended.at[:, columns], dst_ref=attended.at[:, columns],
                send_sem=ag_send.at[split, k], recv_sem=ag_recv.at[split, k],
                device_id=(rep, x_at(step)), device_id_type=MESH,
            )
            copy.start()
            gather.append(copy)
    issue(len(pieces) * CHUNKS)
    for copy in gather:
        copy.wait()
    results[1].start()
    for copy in pairs_sent + metas + asks + answers + scatter + swaps:
        copy.wait_send()
    for copy in bulk + results:
        copy.wait()


def run_layer(queries, new_token_kv, resident_cache, resident_lengths, new_caches, new_lengths, handoff, out_weight):
    count, _, half, wide = new_caches.shape
    width = wide // 2
    groups = lax.axis_size("rep")
    entries = groups * CAP
    rows, depth = queries.shape
    heads = depth // HEAD
    tile = CAP * heads
    pairs = rows * heads
    columns = out_weight.shape[1]
    wide_x = len(X_STEPS) + 1
    block = columns // wide_x
    peers, x_peers = len(REP_STEPS), len(X_STEPS)
    kind = new_caches.dtype
    dma = pltpu.SemaphoreType.DMA
    far = pl.BlockSpec(memory_space=pl.ANY)
    f32 = jnp.float32
    return pl.pallas_call(
        layer_kernel,
        out_shape=(
            jax.ShapeDtypeStruct((rows, columns), kind),
            jax.ShapeDtypeStruct((entries, 2 * half, width), kind),
            jax.ShapeDtypeStruct((8, pairs), jnp.int32),
        ),
        in_specs=[far] * 8,
        out_specs=(far, far, far),
        scratch_shapes=[
            pltpu.VMEM((rows, columns), kind),
            pltpu.VMEM((8, pairs), jnp.int32),
            pltpu.SMEM((1, 2, count), jnp.int32),
            pltpu.SMEM(new_lengths.shape, jnp.int32),
            pltpu.SMEM(resident_lengths.shape, jnp.int32),
            pltpu.VMEM(queries.shape, kind),
            pltpu.VMEM(new_token_kv.shape, kind),
            pltpu.VMEM((groups, 1, HEAD), jnp.int32),
            pltpu.VMEM((groups, 1, HEAD), jnp.int32),
            pltpu.VMEM((count, half, width), kind),
            pltpu.VMEM((count, half, width), kind),
            *[pltpu.VMEM((count, half // CHUNKS, width), kind)] * CHUNKS,
            pltpu.VMEM((groups, CAP, half, width), kind),
            pltpu.VMEM((CHUNKS, groups, CAP, half // CHUNKS, width), kind),
            pltpu.VMEM(resident_cache.shape, kind),
            pltpu.VMEM((wide_x, depth, block), kind),
            pltpu.VMEM((rows, heads, HEAD), f32),
            pltpu.VMEM((groups, tile, HEAD), kind),
            pltpu.VMEM((2, groups, tile, HEAD), kind),
            pltpu.VMEM((2, entries, heads, HEAD), f32),
            pltpu.VMEM((count, tile, HEAD), f32),
            pltpu.VMEM((count, tile, HEAD), f32),
            pltpu.VMEM((2, groups, tile, HEAD), kind),
            pltpu.VMEM((2, groups, tile, HEAD), kind),
            pltpu.VMEM((2, groups, 1, HEAD), f32),
            pltpu.VMEM((2, groups, 1, HEAD), f32),
            pltpu.VMEM((entries * heads, pairs), kind),
            pltpu.VMEM((3, pairs, HEAD), f32),
            pltpu.VMEM((SPLITS, x_peers, rows, block // SPLITS), kind),
            pltpu.VMEM((SPLITS, x_peers, rows, block // SPLITS), kind),
            pltpu.VMEM((SPLITS, 2, rows, block // SPLITS), kind),
            dma((2,)), dma((CHUNKS,)), dma((CHUNKS,)), dma((CHUNKS + 1, peers)), dma((CHUNKS + 1, peers)), dma((CHUNKS + 1,)),
            dma((peers,)), dma((peers,)),
            dma((2, groups)), dma((2, groups)), dma((2, groups)), dma((2, groups)), dma((2, groups)), dma((2, groups)), dma((RES_PARTS,)), dma((wide_x,)),
            dma((SPLITS, x_peers)), dma((SPLITS, x_peers)), dma((SPLITS,)), dma((SPLITS,)), dma((SPLITS, x_peers)), dma((SPLITS, x_peers)),
            dma((5,)), dma((2,)),
        ],
        compiler_params=pltpu.CompilerParams(
            collective_id=0, has_side_effects=True, vmem_limit_bytes=VMEM_BYTES
        ),
        name="layer",
    )(jnp.swapaxes(handoff, 1, 2), new_lengths, resident_lengths, queries, new_token_kv, resident_cache, new_caches, out_weight)


def install_kernel(
    res_len_far, own_kv_far, table, arrived, resident, attended_in, updated, attended, buf, own_now, notes, res_len, own_kv, whole, small_sem, hand_on, get, put
):
    rows, tokens, width = buf.shape
    heads = table.shape[1] // rows
    capacity = arrived.shape[1]
    step = 16
    smalls = []
    for k, (source, target) in enumerate(((table, notes), (res_len_far, res_len), (own_kv_far, own_kv))):
        copy = pltpu.make_async_copy(source, target, small_sem.at[k])
        copy.start()
        smalls.append(copy)
    whole_in = pltpu.make_async_copy(attended_in, whole, hand_on.at[0])
    whole_out = pltpu.make_async_copy(whole, attended, hand_on.at[1])
    whole_in.start()
    smalls[0].wait()

    def entry(r):
        return notes[0, r * heads] - 1

    def get_new(r):
        return pltpu.make_async_copy(arrived.at[entry(r)], buf.at[r, pl.ds(0, capacity), :], get.at[r])

    def get_old(r):
        return pltpu.make_async_copy(resident.at[r], buf.at[r], get.at[r])

    def start(r, carry):
        @pl.when(entry(r) >= 0)
        def _():
            get_new(r).start()
            buf[r, capacity:tokens, :] = jnp.zeros((tokens - capacity, width), buf.dtype)

        @pl.when(entry(r) < 0)
        def _():
            get_old(r).start()
        return carry

    lax.fori_loop(0, rows, start, 0)
    for copy in smalls[1:]:
        copy.wait()
    own_now[...] = own_kv[...].astype(jnp.float32)
    whole_in.wait()
    whole_out.start()
    at = iota((step, width), 0)

    def patch(r, carry):
        token = own_now[pl.ds(r, 1), :]
        new = entry(r) >= 0
        length = jnp.where(new, notes[1, r * heads], res_len[0, r])
        block = length // step
        here = pl.ds(pl.multiple_of(block * step, step), step)

        @pl.when(new)
        def _():
            get_new(r).wait()
            kept = jnp.where(at < length - block * step, buf[r, here, :].astype(jnp.float32), 0.0)
            buf[r, here, :] = jnp.where(at == length - block * step, token, kept).astype(buf.dtype)

            def clear(i, carry):
                buf[r, pl.ds(pl.multiple_of(i * step, step), step), :] = jnp.zeros((step, width), buf.dtype)
                return carry

            lax.fori_loop(block + 1, capacity // step, clear, 0)

        @pl.when(jnp.logical_not(new))
        def _():
            get_old(r).wait()
            kept = buf[r, here, :].astype(jnp.float32)
            buf[r, here, :] = jnp.where(at == length - block * step, token, kept).astype(buf.dtype)

        pltpu.make_async_copy(buf.at[r], updated.at[r], put.at[r]).start()
        return carry

    lax.fori_loop(0, rows, patch, 0)

    def finish(r, carry):
        pltpu.make_async_copy(buf.at[r], updated.at[r], put.at[r]).wait()
        return carry

    lax.fori_loop(0, rows, finish, 0)
    whole_out.wait()


def install(resident_lengths, new_token_kv, table, arrived, resident_cache, attended):
    rows, _, width = resident_cache.shape
    dma = pltpu.SemaphoreType.DMA
    far = pl.BlockSpec(memory_space=pl.ANY)
    return pl.pallas_call(
        install_kernel,
        out_shape=(
            jax.ShapeDtypeStruct(resident_cache.shape, resident_cache.dtype),
            jax.ShapeDtypeStruct(attended.shape, attended.dtype),
        ),
        in_specs=[far] * 6,
        out_specs=(far, far),
        scratch_shapes=[
            pltpu.VMEM(resident_cache.shape, resident_cache.dtype),
            pltpu.VMEM((rows, width), jnp.float32),
            pltpu.SMEM(table.shape, jnp.int32),
            pltpu.SMEM(resident_lengths.shape, jnp.int32),
            pltpu.VMEM(new_token_kv.shape, new_token_kv.dtype),
            pltpu.VMEM(attended.shape, attended.dtype),
            dma((3,)), dma((2,)), dma((rows,)), dma((rows,)),
        ],
        compiler_params=pltpu.CompilerParams(vmem_limit_bytes=VMEM_BYTES),
        name="install",
    )(resident_lengths, new_token_kv, table, arrived, resident_cache, attended)


def body(
    queries,
    new_token_kv,
    resident_cache,
    resident_lengths,
    new_caches,
    new_lengths,
    handoff,
    out_weight,
):
    attended, arrived, table = run_layer(
        queries, new_token_kv, resident_cache, resident_lengths, new_caches, new_lengths, handoff, out_weight
    )
    updated, attended = install(resident_lengths, new_token_kv, table, arrived, resident_cache, attended)
    return (attended, updated)


def solution(mesh):
    placed = (
        P("rep", "tp"),
        P("rep", "tp"),
        P("rep", None, "tp"),
        P("rep", None),
        P("rep", "tp", None, None),
        P("rep", None),
        P("rep", None, None),
        P("tp", None),
    )
    return jax.shard_map(
        body,
        mesh=mesh,
        in_specs=placed,
        out_specs=(P("rep", None), P("rep", None, "tp")),
        check_vma=False,
    )
```

```python
import functools

import jax
import jax.numpy as jnp
from jax import lax
from jax.experimental import pallas as pl
from jax.experimental.pallas import tpu as pltpu
from jax.sharding import PartitionSpec as P

HEAD = 128
CAP = 2
NEG_FILL = -1e30
SCALE = HEAD ** (-0.5)
MESH = pl.DeviceIdType.MESH
NO_ROW = 32
LEN_UNIT = 64
RES_PARTS = 4
VMEM_BYTES = 63 * 2**20
CHUNKS = 4
PORTIONS = (28, 32, 24, 20, 24)
RES_EARLY = 2
EARLY_ROWS = 12
SPLITS = 2

REP_STEPS = [
    (1, 1, 0), (0, 3, 0), (1, 2, 0), (0, 1, 1), (1, 3, 1), (1, 0, 0), (0, 2, 1), (1, 1, 1),
    (0, 3, 1), (1, 2, 1), (0, 1, 0), (1, 3, 0), (1, 0, 1), (0, 2, 0), (0, 0, 1),
]
TP_STEPS = [(h, x) for x in (2, 1, 3, 0) for h in (1, 0) if (h, x) != (0, 0)]
X_STEPS = (2, 1, 3)


def rep_at(rep, step, sign):
    y, z, c = rep // 8, (rep // 2) % 4, rep % 2
    dy, dz, dc = step
    return ((y + dy) % 2) * 8 + ((z + sign * dz + 4) % 4) * 2 + (c + dc) % 2


def tp_at(tp, step, sign):
    h, x = tp // 4, tp % 4
    dh, dx = step
    return ((h + dh) % 2) * 4 + (x + sign * dx + 4) % 4


def iota(shape, dim):
    return lax.broadcasted_iota(jnp.int32, shape, dim)


def contract_last(a, b):
    return lax.dot_general(a, b, (((1,), (1,)), ((), ())), preferred_element_type=jnp.float32)


def contract_first(a, b):
    return lax.dot_general(a, b, (((0,), (0,)), ((), ())), preferred_element_type=jnp.float32)


def attend_pair(query_pair, kv_a, kv_b, limits):
    low = iota(query_pair.shape, 0) < 8
    zero = jnp.zeros_like(query_pair)
    blocks = jnp.concatenate([jnp.where(low, query_pair, zero), jnp.where(low, zero, query_pair)], axis=1)
    keys = jnp.concatenate([kv_a[:, :HEAD], kv_b[:, :HEAD]], axis=1)
    values = jnp.concatenate([kv_a[:, HEAD:], kv_b[:, HEAD:]], axis=1)
    scores = contract_last(blocks.astype(jnp.bfloat16), keys) * SCALE
    allowed = iota(scores.shape, 1) < limits
    peak = jnp.max(jnp.where(allowed, scores, NEG_FILL), axis=1, keepdims=True)
    weights = jnp.where(allowed, jnp.exp(jnp.where(allowed, scores, peak) - peak), 0.0).astype(jnp.bfloat16)
    total = jnp.sum(weights.astype(jnp.float32), axis=1, keepdims=True)
    both = jnp.dot(weights, values, preferred_element_type=jnp.float32)
    return peak, total, jnp.where(low, both[:, :HEAD], both[:, HEAD:])


def combine(peak, total, acc, own_score, own_value):
    top = jnp.maximum(peak, own_score)
    own_weight, factor = jnp.exp(own_score - top), jnp.exp(peak - top)
    return (own_weight * own_value + factor * acc) / (own_weight + factor * total)


def layer_kernel(
    hand_far, new_len_far, res_len_far, queries_far, own_kv_far, resident, caches, weight,
    attended_far, arrived, table_far,
    attended, table, hand, new_len, res_len, queries, own_kv,
    meta_send, meta_all, own, theirs, other0, other1, other2, other3, packed, packed2, res, held, q3, query_out, query_in, query_by, acc_by, note_by, part_out, part_in, note_out, note_in,
    selector, rows3, staged, parts, sums,
    own_sem, pair_send, pair_recv, send, recv, stay, meta_s, meta_r, q_s, q_r, p_s, p_r, n_s, n_r, res_sem, load,
    rs_send, rs_recv, swap_send, swap_recv, ag_send, ag_recv, small_sem, result_sem,
):
    rep, tp = lax.axis_index("rep"), lax.axis_index("tp")
    parity = tp % 2
    partner = tp + 1 - 2 * parity
    count, half, width = own.shape
    row_count = res.shape[0]
    peers = len(REP_STEPS)
    smalls = []
    for k, (source, target) in enumerate(
        ((hand_far, hand), (new_len_far, new_len), (queries_far, queries), (own_kv_far, own_kv), (res_len_far, res_len))
    ):
        copy = pltpu.make_async_copy(source, target, small_sem.at[k])
        copy.start()
        smalls.append(copy)
    mine = pl.ds(pl.multiple_of(parity * width, width), width)
    away = pl.ds(pl.multiple_of((1 - parity) * width, width), width)
    own_loads = [
        pltpu.make_async_copy(caches.at[:, 0, :, mine], own, own_sem.at[0]),
        pltpu.make_async_copy(caches.at[:, 0, :, away], theirs, own_sem.at[1]),
    ]
    for copy in own_loads:
        copy.start()
    res_loads = []
    part_rows = row_count // RES_PARTS
    for k in range(RES_PARTS):
        rows = pl.ds(k * part_rows, part_rows)
        copy = pltpu.make_async_copy(resident.at[rows], res.at[rows], res_sem.at[k])
        copy.start()
        res_loads.append(copy)

    barrier = pltpu.get_barrier_semaphore()
    for step in REP_STEPS:
        for to in (tp, partner):
            pl.semaphore_signal(barrier, inc=1, device_id=(rep_at(rep, step, -1), to), device_id_type=MESH)
    for step in TP_STEPS:
        pl.semaphore_signal(barrier, inc=1, device_id=(rep, tp_at(tp, step, -1)), device_id_type=MESH)

    for copy in smalls[:2]:
        copy.wait()
    targets = [hand[0, 0, i] for i in range(count)]

    def slot_picks(group):
        seen, first, second = jnp.int32(0), jnp.int32(0), jnp.int32(0)
        for i in range(count):
            hit = targets[i] == group
            first = jnp.where(hit & (seen == 0), i, first)
            second = jnp.where(hit & (seen == 1), i, second)
            seen = seen + hit.astype(jnp.int32)
        return first, second, seen

    def code_of(pick, filled):
        return jnp.where(filled, hand[0, 1, pick] + LEN_UNIT * new_len[0, pick], NO_ROW)

    all_steps = REP_STEPS + [(0, 0, 0)]
    picks = []
    code_lane = iota((1, HEAD), 1)
    for k, step in enumerate(all_steps):
        first, second, seen = slot_picks(rep_at(rep, step, 1))
        picks.append((first, second))
        meta_send[k] = jnp.where(code_lane < HEAD // CAP, code_of(first, seen > 0), code_of(second, seen > 1))
    meta_all[rep] = meta_send[peers]
    pl.semaphore_wait(barrier, 2 * len(REP_STEPS) + len(TP_STEPS))

    metas = []
    for k, step in enumerate(REP_STEPS):
        copy = pltpu.make_async_remote_copy(
            src_ref=meta_send.at[k], dst_ref=meta_all.at[rep], send_sem=meta_s.at[k], recv_sem=meta_r.at[k],
            device_id=(rep_at(rep, step, 1), tp), device_id_type=MESH,
        )
        copy.start()
        metas.append(copy)
    pairs_sent = []
    others = (other0, other1, other2, other3)
    span = half // CHUNKS

    def send_chunk():
        c = len(pairs_sent)
        tokens = pl.ds(c * span, span)
        copy = pltpu.make_async_remote_copy(
            src_ref=caches.at[:, 0, tokens, away], dst_ref=others[c],
            send_sem=pair_send.at[c], recv_sem=pair_recv.at[c], device_id=(rep, partner), device_id_type=MESH,
        )
        copy.start()
        pairs_sent.append(copy)

    slots = pl.ds(rep * CAP, CAP)
    bulk = []
    pieces = [(None, k) for k in range(peers + 1)] + [(c, k) for c in range(CHUNKS) for k in range(peers + 1)]

    def issue(units):
        while units > 0 and len(bulk) < len(pieces):
            c, k = pieces[len(bulk)]
            first, second = picks[k]
            if c is None:
                if k == 0:
                    own_loads[0].wait()
                packed[k, 0] = own[first]
                packed[k, 1] = own[second]
                source, sems = packed.at[k], 0
                tokens = pl.ds(pl.multiple_of(parity * half, half), half)
                units -= CHUNKS
            else:
                if k == 0:
                    pairs_sent[c].wait_recv()
                packed2[c, k, 0] = others[c][first]
                packed2[c, k, 1] = others[c][second]
                source, sems = packed2.at[c, k], c + 1
                tokens = pl.ds(pl.multiple_of((1 - parity) * half + c * span, span), span)
                units -= 1
            if k < peers:
                copy = pltpu.make_async_remote_copy(
                    src_ref=source, dst_ref=arrived.at[slots, tokens, :], send_sem=send.at[sems, k], recv_sem=recv.at[sems, k],
                    device_id=(rep_at(rep, all_steps[k], 1), tp), device_id_type=MESH,
                )
            else:
                copy = pltpu.make_async_copy(source, arrived.at[slots, tokens, :], stay.at[sems])
            copy.start()
            bulk.append(copy)

    send_chunk()
    issue(PORTIONS[0])

    for copy in smalls[2:]:
        copy.wait()
    heads = queries.shape[1] // HEAD
    for j in range(heads):
        q3[:, j, :] = queries[:, j * HEAD:(j + 1) * HEAD].astype(jnp.float32)
    pairs = row_count * heads
    tile = CAP * heads
    q_rows = q3[...].reshape(pairs, HEAD)
    own_now = own_kv[...].astype(jnp.float32)
    own_rows = jnp.broadcast_to(own_now[:, None, :], (row_count, heads, width)).reshape(pairs, width)

    for copy in metas:
        copy.wait_recv()
    codes = meta_all[...]
    codes = jnp.stack(
        [jnp.broadcast_to(codes[:, :, at:at + 1], (peers + 1, heads, HEAD)) for at in range(0, HEAD, HEAD // CAP)], axis=1
    ).reshape(pairs, HEAD)
    row_of = codes % LEN_UNIT
    lane, sub = iota((pairs, HEAD), 1), iota((pairs, HEAD), 0)
    lanes_rows = HEAD // heads
    for b in range(row_count // lanes_rows):
        hit = (row_of == b * lanes_rows + lane // heads) & (lane % heads == sub % heads)
        selector[:, b * HEAD:(b + 1) * HEAD] = hit.astype(jnp.float32).astype(jnp.bfloat16)
    picked = jnp.dot(selector[...], q_rows.astype(jnp.bfloat16), preferred_element_type=jnp.float32)
    query_out[...] = picked.astype(jnp.bfloat16).reshape(peers + 1, tile, HEAD)
    query_in[0, rep] = query_out[rep]
    asks = []
    for k, step in enumerate(all_steps):
        group = rep_at(rep, step, 1)
        for w, to in ((0, tp), (1, partner)):
            if k == peers and w == 0:
                continue
            copy = pltpu.make_async_remote_copy(
                src_ref=query_out.at[group], dst_ref=query_in.at[w, rep], send_sem=q_s.at[w, k], recv_sem=q_r.at[w, k],
                device_id=(group, to), device_id_type=MESH,
            )
            copy.start()
            asks.append(copy)
    send_chunk()
    send_chunk()
    issue(PORTIONS[1])

    low_col = iota((tile, 1), 0) < heads

    def resident_pair(i, carry):
        a, b = 2 * i, 2 * i + 1
        limits = jnp.where(low_col, res_len[0, a], res_len[0, b])
        peak, total, acc = attend_pair(q3[pl.ds(a, 2)].reshape(tile, HEAD), res[a], res[b], limits)
        at = pl.ds(pl.multiple_of(i * tile, tile), tile)
        rows3[0, at, :] = jnp.broadcast_to(peak, acc.shape)
        rows3[1, at, :] = jnp.broadcast_to(total, acc.shape)
        rows3[2, at, :] = acc
        return carry

    def resident_part(k):
        res_loads[k].wait()
        lax.fori_loop(k * part_rows // 2, (k + 1) * part_rows // 2, resident_pair, 0)

    for k in range(RES_EARLY):
        resident_part(k)

    for copy in asks:
        copy.wait_recv()
    own_loads[1].wait()
    query_by[...] = query_in[...].astype(jnp.float32).reshape(query_by.shape)

    for i in range(count):
        at = targets[i] * CAP + sum([(targets[n] == targets[i]).astype(jnp.int32) for n in range(i)], jnp.int32(0))
        asked = jnp.concatenate([query_by[0, at], query_by[1, at]], axis=0)
        peak, total, acc = attend_pair(asked, own[i], theirs[i], new_len[0, i] - half * parity)
        acc_by[i] = acc
        peak, total = jnp.broadcast_to(peak, acc.shape), jnp.broadcast_to(total, acc.shape)
        note_by[i] = jnp.where(iota(acc.shape, 1) % 2 == 0, peak, total)
    note_lane, note_sub = iota((heads, HEAD), 1), iota((heads, HEAD), 0)
    answers = []
    for k, step in enumerate(all_steps):
        first, second = picks[k]
        group = rep_at(rep, step, 1)
        for w, to in ((0, tp), (1, partner)):
            of = slice(w * heads, (w + 1) * heads)
            both = jnp.concatenate([acc_by[first][of], acc_by[second][of]], axis=0).astype(part_out.dtype)
            note = jnp.where(note_lane % 4 < 2, note_by[first][of], note_by[second][of])
            note = jnp.sum(jnp.where(note_lane // 4 == note_sub, note, 0.0), axis=0, keepdims=True)
            if k == peers and w == 0:
                part_in[0, rep] = both
                note_in[0, rep] = note
                continue
            part_out[w, k] = both
            note_out[w, k] = note
            for source, target, out_sem, in_sem in ((part_out, part_in, p_s, p_r), (note_out, note_in, n_s, n_r)):
                copy = pltpu.make_async_remote_copy(
                    src_ref=source.at[w, k], dst_ref=target.at[w, rep], send_sem=out_sem.at[w, k], recv_sem=in_sem.at[w, k],
                    device_id=(group, to), device_id_type=MESH,
                )
                copy.start()
                answers.append(copy)
    send_chunk()
    issue(PORTIONS[2])
    here = tp % 4
    block = held.shape[2]
    w_loads = []
    for k, step in enumerate(X_STEPS + (0,)):
        at = pl.multiple_of(((here + step) % 4) * block, block)
        copy = pltpu.make_async_copy(weight.at[:, pl.ds(at, block)], held.at[k], load.at[k])
        copy.start()
        w_loads.append(copy)

    for k in range(RES_EARLY, RES_PARTS):
        resident_part(k)
    row_score = jnp.sum(q_rows * own_rows[:, :HEAD], axis=1, keepdims=True) * SCALE
    rows3[2] = combine(rows3[0], rows3[1], rows3[2], row_score, own_rows[:, HEAD:])
    picked_kv = jnp.dot(selector[...], own_rows.astype(jnp.bfloat16), preferred_element_type=jnp.float32)
    entry_score = jnp.sum(picked * picked_kv[:, :HEAD], axis=1, keepdims=True) * SCALE
    taken = contract_first(selector[...], jnp.ones((pairs, HEAD), jnp.bfloat16))
    entry_of = (sub // heads + 1).astype(jnp.float32)
    notes = jnp.where(lane == 0, entry_of, jnp.where(lane == 1, (codes // LEN_UNIT).astype(jnp.float32), 0.0))
    table[...] = contract_first(notes.astype(jnp.bfloat16), selector[...])[0:8, :].astype(jnp.int32)
    results = [
        pltpu.make_async_copy(table, table_far, result_sem.at[0]),
        pltpu.make_async_copy(attended, attended_far, result_sem.at[1]),
    ]
    results[0].start()

    for copy in answers:
        copy.wait_recv()
    peaks, totals, accs = [], [], []
    cell, cell_sub = iota((peers + 1, heads, HEAD), 2), iota((peers + 1, heads, HEAD), 1)
    for w in range(CAP):
        accs.append(part_in[w].astype(jnp.float32).reshape(pairs, HEAD))
        note = jnp.broadcast_to(note_in[w], cell.shape)

        def column(at):
            found = jnp.sum(jnp.where(cell == 4 * cell_sub + at, note, 0.0), axis=2, keepdims=True)
            return jnp.broadcast_to(found, cell.shape)

        peaks.append(jnp.stack([column(0), column(2)], axis=1).reshape(pairs, HEAD))
        totals.append(jnp.stack([column(1), column(3)], axis=1).reshape(pairs, HEAD))
    top = jnp.maximum(jnp.maximum(peaks[0], peaks[1]), entry_score)
    own_weight = jnp.exp(entry_score - top)
    factors = [jnp.exp(peak - top) for peak in peaks]
    above = own_weight * picked_kv[:, HEAD:] + factors[0] * accs[0] + factors[1] * accs[1]
    below = own_weight + factors[0] * totals[0] + factors[1] * totals[1]
    moved = contract_first(selector[...], (above / below).astype(jnp.bfloat16))
    q3[...] = jnp.where(taken > 0.5, moved, rows3[2]).reshape(row_count, heads, HEAD)
    attention = jnp.concatenate([q3[:, j, :] for j in range(heads)], axis=1).astype(jnp.bfloat16)

    def x_at(step):
        return (tp // 4) * 4 + (here + step) % 4

    last = len(X_STEPS)
    part_width = block // SPLITS

    def share(k, split):
        at = slice(split * part_width, (split + 1) * part_width)
        return jnp.dot(attention, held[k, :, at], preferred_element_type=jnp.float32)

    scatter = []
    for split in range(SPLITS):
        for k, step in enumerate(X_STEPS):
            if split == 0:
                w_loads[k].wait()
            staged[split, k] = share(k, split).astype(staged.dtype)
            copy = pltpu.make_async_remote_copy(
                src_ref=staged.at[split, k], dst_ref=parts.at[split, k],
                send_sem=rs_send.at[split, k], recv_sem=rs_recv.at[split, k],
                device_id=(rep, x_at(step)), device_id_type=MESH,
            )
            copy.start()
            scatter.append(copy)
    issue(PORTIONS[3])
    w_loads[last].wait()
    swaps = []
    for split in range(SPLITS):
        total = share(last, split)
        for k in range(last):
            scatter[split * last + k].wait_recv()
            total = total + parts[split, k].astype(jnp.float32)
        sums[split, 0] = total.astype(sums.dtype)
        copy = pltpu.make_async_remote_copy(
            src_ref=sums.at[split, 0], dst_ref=sums.at[split, 1], send_sem=swap_send.at[split], recv_sem=swap_recv.at[split],
            device_id=(rep, (tp + 4) % 8), device_id_type=MESH,
        )
        copy.start()
        swaps.append(copy)
    issue(PORTIONS[4])
    gather = []
    for split in range(SPLITS):
        swaps[split].wait_recv()
        columns = pl.ds(pl.multiple_of(here * block + split * part_width, part_width), part_width)
        both = sums[split, 0].astype(jnp.float32) + sums[split, 1].astype(jnp.float32)
        attended[:, columns] = both.astype(attended.dtype)
        for k, step in enumerate(X_STEPS):
            copy = pltpu.make_async_remote_copy(
                src_ref=attended.at[:, columns], dst_ref=attended.at[:, columns],
                send_sem=ag_send.at[split, k], recv_sem=ag_recv.at[split, k],
                device_id=(rep, x_at(step)), device_id_type=MESH,
            )
            copy.start()
            gather.append(copy)
    issue(len(pieces) * CHUNKS)
    for copy in gather:
        copy.wait()
    results[1].start()
    for copy in pairs_sent + metas + asks + answers + scatter + swaps:
        copy.wait_send()
    for copy in bulk + results:
        copy.wait()


def run_layer(queries, new_token_kv, resident_cache, resident_lengths, new_caches, new_lengths, handoff, out_weight):
    count, _, half, wide = new_caches.shape
    width = wide // 2
    groups = lax.axis_size("rep")
    entries = groups * CAP
    rows, depth = queries.shape
    heads = depth // HEAD
    tile = CAP * heads
    pairs = rows * heads
    columns = out_weight.shape[1]
    wide_x = len(X_STEPS) + 1
    block = columns // wide_x
    peers, x_peers = len(REP_STEPS), len(X_STEPS)
    kind = new_caches.dtype
    dma = pltpu.SemaphoreType.DMA
    far = pl.BlockSpec(memory_space=pl.ANY)
    f32 = jnp.float32
    return pl.pallas_call(
        layer_kernel,
        out_shape=(
            jax.ShapeDtypeStruct((rows, columns), kind),
            jax.ShapeDtypeStruct((entries, 2 * half, width), kind),
            jax.ShapeDtypeStruct((8, pairs), jnp.int32),
        ),
        in_specs=[far] * 8,
        out_specs=(far, far, far),
        scratch_shapes=[
            pltpu.VMEM((rows, columns), kind),
            pltpu.VMEM((8, pairs), jnp.int32),
            pltpu.SMEM((1, 2, count), jnp.int32),
            pltpu.SMEM(new_lengths.shape, jnp.int32),
            pltpu.SMEM(resident_lengths.shape, jnp.int32),
            pltpu.VMEM(queries.shape, kind),
            pltpu.VMEM(new_token_kv.shape, kind),
            pltpu.VMEM((groups, 1, HEAD), jnp.int32),
            pltpu.VMEM((groups, 1, HEAD), jnp.int32),
            pltpu.VMEM((count, half, width), kind),
            pltpu.VMEM((count, half, width), kind),
            *[pltpu.VMEM((count, half // CHUNKS, width), kind)] * CHUNKS,
            pltpu.VMEM((groups, CAP, half, width), kind),
            pltpu.VMEM((CHUNKS, groups, CAP, half // CHUNKS, width), kind),
            pltpu.VMEM(resident_cache.shape, kind),
            pltpu.VMEM((wide_x, depth, block), kind),
            pltpu.VMEM((rows, heads, HEAD), f32),
            pltpu.VMEM((groups, tile, HEAD), kind),
            pltpu.VMEM((2, groups, tile, HEAD), kind),
            pltpu.VMEM((2, entries, heads, HEAD), f32),
            pltpu.VMEM((count, tile, HEAD), f32),
            pltpu.VMEM((count, tile, HEAD), f32),
            pltpu.VMEM((2, groups, tile, HEAD), kind),
            pltpu.VMEM((2, groups, tile, HEAD), kind),
            pltpu.VMEM((2, groups, 1, HEAD), f32),
            pltpu.VMEM((2, groups, 1, HEAD), f32),
            pltpu.VMEM((entries * heads, pairs), kind),
            pltpu.VMEM((3, pairs, HEAD), f32),
            pltpu.VMEM((SPLITS, x_peers, rows, block // SPLITS), kind),
            pltpu.VMEM((SPLITS, x_peers, rows, block // SPLITS), kind),
            pltpu.VMEM((SPLITS, 2, rows, block // SPLITS), kind),
            dma((2,)), dma((CHUNKS,)), dma((CHUNKS,)), dma((CHUNKS + 1, peers)), dma((CHUNKS + 1, peers)), dma((CHUNKS + 1,)),
            dma((peers,)), dma((peers,)),
            dma((2, groups)), dma((2, groups)), dma((2, groups)), dma((2, groups)), dma((2, groups)), dma((2, groups)), dma((RES_PARTS,)), dma((wide_x,)),
            dma((SPLITS, x_peers)), dma((SPLITS, x_peers)), dma((SPLITS,)), dma((SPLITS,)), dma((SPLITS, x_peers)), dma((SPLITS, x_peers)),
            dma((5,)), dma((2,)),
        ],
        compiler_params=pltpu.CompilerParams(
            collective_id=0, has_side_effects=True, vmem_limit_bytes=VMEM_BYTES
        ),
        name="layer",
    )(jnp.swapaxes(handoff, 1, 2), new_lengths, resident_lengths, queries, new_token_kv, resident_cache, new_caches, out_weight)


def install_kernel(
    res_len_far, own_kv_far, table, arrived, resident, attended_in, updated, attended, buf, alt, own_now, notes, res_len, own_kv, whole, small_sem, hand_on, get, fresh, put
):
    rows, tokens, width = buf.shape
    heads = table.shape[1] // rows
    capacity = arrived.shape[1]
    step = 16
    smalls = []
    for k, (source, target) in enumerate(((table, notes), (res_len_far, res_len), (own_kv_far, own_kv))):
        copy = pltpu.make_async_copy(source, target, small_sem.at[k])
        copy.start()
        smalls.append(copy)
    whole_in = pltpu.make_async_copy(attended_in, whole, hand_on.at[0])
    whole_out = pltpu.make_async_copy(whole, attended, hand_on.at[1])
    whole_in.start()

    def early(r, carry):
        pltpu.make_async_copy(resident.at[r], buf.at[r], get.at[r]).start()
        return carry

    lax.fori_loop(0, EARLY_ROWS, early, 0)
    smalls[0].wait()

    def entry(r):
        return notes[0, r * heads] - 1

    def get_new(r):
        return pltpu.make_async_copy(arrived.at[entry(r)], alt.at[r, pl.ds(0, capacity), :], fresh.at[r])

    def get_old(r):
        return pltpu.make_async_copy(resident.at[r], buf.at[r], get.at[r])

    def start(r, carry):
        @pl.when(entry(r) >= 0)
        def _():
            get_new(r).start()
            alt[r, capacity:tokens, :] = jnp.zeros((tokens - capacity, width), buf.dtype)

        @pl.when((entry(r) < 0) & (r >= EARLY_ROWS))
        def _():
            get_old(r).start()
        return carry

    lax.fori_loop(0, rows, start, 0)
    for copy in smalls[1:]:
        copy.wait()
    own_now[...] = own_kv[...].astype(jnp.float32)
    whole_in.wait()
    whole_out.start()
    at = iota((step, width), 0)

    def patch(r, carry):
        token = own_now[pl.ds(r, 1), :]
        new = entry(r) >= 0
        length = jnp.where(new, notes[1, r * heads], res_len[0, r])
        block = length // step
        here = pl.ds(pl.multiple_of(block * step, step), step)

        @pl.when(new)
        def _():
            get_new(r).wait()
            kept = jnp.where(at < length - block * step, alt[r, here, :].astype(jnp.float32), 0.0)
            alt[r, here, :] = jnp.where(at == length - block * step, token, kept).astype(buf.dtype)

            def clear(i, carry):
                alt[r, pl.ds(pl.multiple_of(i * step, step), step), :] = jnp.zeros((step, width), buf.dtype)
                return carry

            lax.fori_loop(block + 1, capacity // step, clear, 0)
            pltpu.make_async_copy(alt.at[r], updated.at[r], put.at[r]).start()

        @pl.when(jnp.logical_not(new))
        def _():
            get_old(r).wait()
            kept = buf[r, here, :].astype(jnp.float32)
            buf[r, here, :] = jnp.where(at == length - block * step, token, kept).astype(buf.dtype)
            pltpu.make_async_copy(buf.at[r], updated.at[r], put.at[r]).start()

        return carry

    lax.fori_loop(0, rows, patch, 0)

    def finish(r, carry):
        pltpu.make_async_copy(buf.at[r], updated.at[r], put.at[r]).wait()

        @pl.when((entry(r) >= 0) & (r < EARLY_ROWS))
        def _():
            get_old(r).wait()

        return carry

    lax.fori_loop(0, rows, finish, 0)
    whole_out.wait()


def install(resident_lengths, new_token_kv, table, arrived, resident_cache, attended):
    rows, _, width = resident_cache.shape
    dma = pltpu.SemaphoreType.DMA
    far = pl.BlockSpec(memory_space=pl.ANY)
    return pl.pallas_call(
        install_kernel,
        out_shape=(
            jax.ShapeDtypeStruct(resident_cache.shape, resident_cache.dtype),
            jax.ShapeDtypeStruct(attended.shape, attended.dtype),
        ),
        in_specs=[far] * 6,
        out_specs=(far, far),
        scratch_shapes=[
            pltpu.VMEM(resident_cache.shape, resident_cache.dtype),
            pltpu.VMEM(resident_cache.shape, resident_cache.dtype),
            pltpu.VMEM((rows, width), jnp.float32),
            pltpu.SMEM(table.shape, jnp.int32),
            pltpu.SMEM(resident_lengths.shape, jnp.int32),
            pltpu.VMEM(new_token_kv.shape, new_token_kv.dtype),
            pltpu.VMEM(attended.shape, attended.dtype),
            dma((3,)), dma((2,)), dma((rows,)), dma((rows,)), dma((rows,)),
        ],
        compiler_params=pltpu.CompilerParams(vmem_limit_bytes=VMEM_BYTES),
        name="install",
    )(resident_lengths, new_token_kv, table, arrived, resident_cache, attended)


def body(
    queries,
    new_token_kv,
    resident_cache,
    resident_lengths,
    new_caches,
    new_lengths,
    handoff,
    out_weight,
):
    attended, arrived, table = run_layer(
        queries, new_token_kv, resident_cache, resident_lengths, new_caches, new_lengths, handoff, out_weight
    )
    updated, attended = install(resident_lengths, new_token_kv, table, arrived, resident_cache, attended)
    return (attended, updated)


def solution(mesh):
    placed = (
        P("rep", "tp"),
        P("rep", "tp"),
        P("rep", None, "tp"),
        P("rep", None),
        P("rep", "tp", None, None),
        P("rep", None),
        P("rep", None, None),
        P("tp", None),
    )
    return jax.shard_map(
        body,
        mesh=mesh,
        in_specs=placed,
        out_specs=(P("rep", None), P("rep", None, "tp")),
        check_vma=False,
    )
```
